32 devices in a mesh: ctx: 16 (over z, y, core), head: 2 (over x).
Axes of the slice: x: 2, y: 2, z: 4, core: 2. Of those that a mesh axis runs over, the one named last changes fastest.
Arguments:
- queries: bfloat16 [2048, 64, 128], P('ctx', 'head'), may hold values from -200 to 200
- new_keys: bfloat16 [2048, 8, 128], P('ctx', 'head'), may hold values from -6 to 6
- new_values: bfloat16 [2048, 8, 128], P('ctx', 'head'), may hold values from -6 to 6
- pool_keys: bfloat16 [128, 32, 8, 128], P('ctx', None, 'head'), may hold values from -6 to 6
- pool_values: bfloat16 [128, 32, 8, 128], P('ctx', None, 'head'), may hold values from -6 to 6
- o_weight: bfloat16 [8192, 8192], P('head', 'ctx'), may hold values from -1.5 to 1.5
- page_list: int32 [32], replicated, may hold values from 0 to 127, as said below
Outputs:
- projected: bfloat16 [2048, 8192], P('ctx', 'head')
The draws below stay inside these ranges and needn't reach their ends.
Inputs may be any that keep to these rules, and one draw needn't show every extreme that they name: page_list names 32 distinct pool slots; slot p lies on cycle position p // 8; one cycle position holds exactly 4 of them and none holds more; some hold none.
All inputs are finite; a program needn't handle non-finite values.
Results may differ from the reference program's by a relative error of at most 0.015.
Values may be sent and summed in bfloat16 or wider, within the bound.
No kernel may reach another device: no remote copies, remote signals or barrier semaphores. Data moves between devices by JAX's collectives and lax.ppermute only.
A program may use at most 192 MiB of HBM per device.

```python
import math
import jax
import jax.numpy as jnp
from jax import lax

D = 8192
QH = 64
KVH = 8
HD = 128
PAGE = 32
PG_DEV = 2
SLOTS = 8
OWNERS = 16
PAGES = 32
POOL = 128
PREFIX = 1024
SPAN = 2048


def drawn_pair(key):
    base = jax.random.fold_in(key, 11)
    first, second = jax.random.split(base, 2)
    queries = jnp.clip(jax.random.normal(first, (SPAN, QH, HD), jnp.float32), -5.0, 5.0)
    keys = jnp.clip(jax.random.normal(second, (SPAN, KVH, HD), jnp.float32), -5.0, 5.0)
    return (queries, keys)


def draw_queries(key, part):
    queries, keys = drawn_pair(key)
    return queries.astype(jnp.bfloat16)


def draw_new_keys(key, part):
    queries, keys = drawn_pair(key)
    return keys.astype(jnp.bfloat16)


def draw_page_list(key, part):
    first, second, third, fourth = jax.random.split(jax.random.fold_in(key, 23), 4)
    order = jax.random.permutation(first, OWNERS)
    moves = jax.random.randint(second, (OWNERS // 2,), 0, PG_DEV + 1)
    moves = moves.at[0].set(PG_DEV)
    pair_counts = jnp.stack([PG_DEV + moves, PG_DEV - moves], axis=1).reshape(OWNERS)
    counts = jnp.zeros((OWNERS,), jnp.int32).at[order].set(pair_counts.astype(jnp.int32))
    slot_score = jax.random.randint(third, (OWNERS, SLOTS), 0, 1024) * SLOTS + jnp.arange(SLOTS)[None, :]
    permuted = jnp.argsort(slot_score, axis=1)
    ranks = jnp.argsort(permuted, axis=1)
    live = ranks < counts[:, None]
    slot_ids = (jnp.arange(OWNERS)[:, None] * SLOTS + jnp.arange(SLOTS)[None, :]).reshape(POOL)
    shuffle = jax.random.randint(fourth, (POOL,), 0, 1024)
    ranking = (1 - live.reshape(POOL).astype(jnp.int32)) * (1 << 22) + shuffle * POOL + slot_ids
    picked = jnp.argsort(ranking)[:PAGES]
    return slot_ids[picked].astype(jnp.int32)


def spiked(array, key, source, target, shards_of, factor):
    def block_of(dim):
        return (jnp.arange(array.shape[dim]) // (array.shape[dim] // shards_of)).reshape((-1,) + (1,) * (array.ndim - 1 - dim))

    one_side = jax.random.permutation(key, shards_of)[block_of(target)]
    second = (block_of(target) + shards_of // 2) % shards_of
    return jnp.where((block_of(source) == one_side) | (block_of(source) == second), factor * array, array)


def steps_of(rng, dims, shards, least, high):
    def one(position, parts):
        heights = jax.random.uniform(jax.random.fold_in(jax.random.fold_in(rng, 6), position), (parts,), jnp.float32, least / len(shards), high / len(shards))
        return jnp.repeat(jnp.exp(heights), dims[position] // parts).reshape((-1,) + (1,) * (len(dims) - position - 1))

    factor_of = one(*shards[0])
    for cut in shards[1:]:
        factor_of = factor_of * one(*cut)
    return factor_of


def bell_draw(own_key, dims, deviation, bound, pieces=(), held_as=jnp.bfloat16):
    array = jax.random.normal(own_key, dims, jnp.float32) * deviation
    if len(pieces) > 0:
        array = steps_of(own_key, dims, pieces, -0.22, 0.18) * array
    return jnp.clip(array, min=-bound, max=bound).astype(held_as)


def noise_with(own_key, dims, deviation, limit, pieces, heavy, kind=jnp.bfloat16):
    drawn = deviation * jax.random.normal(own_key, dims, jnp.float32)
    if pieces:
        drawn = drawn * steps_of(own_key, dims, pieces, -0.22, 0.18)
    return jnp.clip(spiked(drawn, jax.random.fold_in(own_key, 3), *heavy), -limit, limit).astype(kind)


def setup_inputs(seed: int = 0) -> dict:
    key_list = jax.random.split(jax.random.key(seed), 8)
    return {
        "queries": draw_queries(jax.random.fold_in(key_list[7], 71), 0),
        "new_keys": draw_new_keys(jax.random.fold_in(key_list[7], 71), 0),
        "new_values": bell_draw(key_list[2], (SPAN, KVH, HD), 1.0, 6.0, ((0, 16), (1, 2))),
        "pool_keys": bell_draw(key_list[3], (POOL, PAGE, KVH, HD), 1.0, 6.0, ((0, 16), (2, 2))),
        "pool_values": bell_draw(key_list[4], (POOL, PAGE, KVH, HD), 1.0, 6.0, ((0, 16), (2, 2))),
        "o_weight": noise_with(key_list[5], (QH * HD, D), (QH * HD // 256) ** -0.5, 1.5, ((0, 2), (1, 16)), (0, 1, 16, 2.0)),
        "page_list": draw_page_list(jax.random.fold_in(key_list[7], 71), 0),
    }


NEG = -1e+30

def reference(queries, new_keys, new_values, pool_keys, pool_values, o_weight, page_list):
    group = QH // KVH
    scale = 1.0 / math.sqrt(HD)
    prefix_keys = jnp.take(pool_keys, page_list, axis=0).reshape(PREFIX, KVH, HD)
    prefix_values = jnp.take(pool_values, page_list, axis=0).reshape(PREFIX, KVH, HD)
    all_keys = jnp.concatenate([prefix_keys, new_keys], axis=0).astype(jnp.float32)
    all_values = jnp.concatenate([prefix_values, new_values], axis=0).astype(jnp.float32)
    block = math.gcd(256, SPAN)
    positions = jnp.arange(PREFIX + SPAN).astype(jnp.int32)

    def one_block(index):
        start = (index * block).astype(jnp.int32)
        query_block = lax.dynamic_slice_in_dim(queries, start, block, 0).astype(jnp.float32)
        query_block = query_block.reshape(block, KVH, group, HD)
        scores = jnp.einsum('rkgd,skd->kgrs', query_block, all_keys) * scale
        rows = PREFIX + start + jnp.arange(block).astype(jnp.int32)
        seen = positions[None, :] <= rows[:, None]
        scores = jnp.where(seen, scores, NEG)
        top = lax.optimization_barrier(jnp.max(scores, axis=-1, keepdims=True))
        weights = jnp.where(seen, jnp.exp(scores - top), 0.0)
        total = lax.optimization_barrier(jnp.sum(weights, axis=-1))
        rounded = lax.optimization_barrier(weights.astype(jnp.bfloat16)).astype(jnp.float32)
        mixed = jnp.einsum('kgrs,skd->kgrd', rounded, all_values) / total[..., None]
        return mixed.transpose(2, 0, 1, 3).reshape(block, QH * HD).astype(jnp.bfloat16)
    attended = lax.map(one_block, jnp.arange(SPAN // block).astype(jnp.int32)).reshape(SPAN, QH * HD)
    return jnp.dot(attended, o_weight, preferred_element_type=jnp.float32).astype(jnp.bfloat16)
```

```python
import functools
import math

import jax
import jax.numpy as jnp
from jax import lax
from jax.experimental import pallas as pl
from jax.experimental.pallas import tpu as pltpu
from jax.sharding import PartitionSpec as P

CORES = 2
LINES = 2
NEG = -1e30
VMEM_LIMIT = 48 * 1024 * 1024


def cycle_of(sites):
    length = sites // LINES
    order = []
    for line in range(LINES):
        steps = range(length) if line % 2 == 0 else range(length - 1, -1, -1)
        order += [z * LINES + line for z in steps]
    return order


def place_of(site, sites):
    z, line = site // LINES, site % LINES
    length = sites // LINES
    return jnp.where(line == 0, z, 2 * length - 1 - z)


def site_perm(sites, shift):
    order = cycle_of(sites)
    return [
        (order[i] * CORES + k, order[(i + shift) % sites] * CORES + k)
        for i in range(sites)
        for k in range(CORES)
    ]


def core_swap(x, count):
    return lax.ppermute(x, "ctx", [(i, i ^ 1) for i in range(count)])


def ring_gather(block, sites):
    ahead = site_perm(sites, 1)
    back = site_perm(sites, -1)
    blocks = {0: [block]}
    f = b = block
    for step in range(1, (sites - 1) // 2 + 1):
        f = lax.ppermute(f, "ctx", ahead)
        b = lax.ppermute(b, "ctx", back)
        blocks[step] = [f]
        blocks[sites - step] = [b]
    if sites % 2 == 0:
        half = block.shape[0] // 2
        blocks[sites // 2] = [
            lax.ppermute(f[:half], "ctx", ahead),
            lax.ppermute(b[half:], "ctx", back),
        ]
    return blocks


def pack_kernel(slots, pages_ref, me_ref, nk_ref, nv_ref, pk_ref, pv_ref, out_ref):
    rows = nk_ref.shape[0]
    page = pk_ref.shape[1]
    kept = (out_ref.shape[0] // 2 - rows) // page
    half = out_ref.shape[0] // 2
    out_ref[...] = jnp.zeros_like(out_ref)
    out_ref[0:rows, :] = nk_ref[...]
    out_ref[half : half + rows, :] = nv_ref[...]
    me = me_ref[0]

    def one(p, count):
        slot = pages_ref[p]
        mine = slot // slots == me

        @pl.when(jnp.logical_and(mine, count < kept))
        def _():
            local = slot % slots
            at = pl.multiple_of(rows + count * page, page)
            out_ref[pl.ds(at, page), :] = pk_ref[local]
            out_ref[pl.ds(pl.multiple_of(half + at, page), page), :] = pv_ref[local]

        return count + mine.astype(jnp.int32)

    lax.fori_loop(0, pages_ref.shape[0], one, jnp.int32(0))


def attend_kernel(cfg, pages_ref, me_ref, q_ref, *refs):
    n, rows, kvheads, group, width, page, slots, kept, key_block = cfg
    sites = n // CORES
    length = sites // LINES
    ins, (o_ref, kbuf, vbuf, table, counts, sem) = refs[:-6], refs[-6:]
    npages = pages_ref.shape[0]
    prefix = npages * page
    me = me_ref[0]
    my_site, my_core = me // CORES, me % CORES
    my_place = jnp.where(my_site % LINES == 0, my_site // LINES, 2 * length - 1 - my_site // LINES)

    for i in range(n):
        counts[i] = 0

    def note(p, _):
        owner = pages_ref[p] // slots
        j = counts[owner]
        table[owner * kept + jnp.minimum(j, kept - 1)] = p
        counts[owner] = j + 1
        return 0

    lax.fori_loop(0, npages, note, 0)

    def copies(go):
        for d in range(sites):
            for swap in range(CORES):
                k_ref, k_at, v_ref, v_at = ins[d * CORES + swap]
                place = lax.rem(my_place + sites - d, sites)
                line = place // length
                z = jnp.where(line == 0, place, 2 * length - 1 - place)
                owner = (z * LINES + line) * CORES + lax.rem(my_core + swap, CORES)
                at = pl.multiple_of(prefix + owner * rows, rows)
                for src, off, dst in ((k_ref, k_at, kbuf), (v_ref, v_at, vbuf)):
                    go(src.at[pl.ds(off, rows)], dst.at[pl.ds(at, rows)])
                for j in range(kept):

                    @pl.when(j < counts[owner])
                    def _():
                        to = pl.multiple_of(table[owner * kept + j] * page, page)
                        for src, off, dst in ((k_ref, k_at, kbuf), (v_ref, v_at, vbuf)):
                            go(src.at[pl.ds(off + rows + j * page, page)], dst.at[pl.ds(to, page)])

    copies(lambda s, t: pltpu.make_async_copy(s, t, sem).start())
    copies(lambda s, t: pltpu.make_async_copy(s, t, sem).wait())

    pair = 2 if group % 2 == 0 else 1
    scale = math.log2(math.e) * width ** (-0.5)
    seen_all = prefix + me * rows
    full = seen_all // key_block

    def one(index, _):
        h = index // (group // pair)
        first = index * pair
        lane = pl.multiple_of(h * width, width)
        q = jnp.concatenate(
            [
                q_ref[:, pl.ds(pl.multiple_of((first + g) * width, width), width)]
                for g in range(pair)
            ],
            axis=0,
        )

        def step(kb, carry, masked):
            top, total, acc = carry
            at = pl.multiple_of(kb * key_block, key_block)
            k = kbuf[pl.ds(at, key_block), pl.ds(lane, width)]
            v = vbuf[pl.ds(at, key_block), pl.ds(lane, width)]
            s = lax.dot_general(q, k, (((1,), (1,)), ((), ())), preferred_element_type=jnp.float32)
            if masked:
                shape = (rows, key_block)
                row = lax.broadcasted_iota(jnp.int32, shape, 0)
                col = lax.broadcasted_iota(jnp.int32, shape, 1)
                seen = col - row <= seen_all - at
                seen = jnp.concatenate([seen] * pair, axis=0)
                s = jnp.where(seen, s, NEG)
            fresh = jnp.maximum(top, jnp.max(s, axis=1, keepdims=True))
            w = jnp.exp2((s - fresh) * scale)
            left = jnp.exp2((top - fresh) * scale)
            total = total * left + jnp.sum(w, axis=1, keepdims=True)
            acc = acc * left + jnp.dot(
                w.astype(jnp.bfloat16), v, preferred_element_type=jnp.float32
            )
            return fresh, total, acc

        carry = (
            jnp.full((pair * rows, 1), NEG, jnp.float32),
            jnp.zeros((pair * rows, 1), jnp.float32),
            jnp.zeros((pair * rows, width), jnp.float32),
        )
        carry = lax.fori_loop(0, full, lambda kb, c: step(kb, c, False), carry)
        top, total, acc = step(full, carry, True)
        out = (acc / total).astype(jnp.bfloat16)
        for g in range(pair):
            o_ref[:, pl.ds(pl.multiple_of((first + g) * width, width), width)] = out[
                g * rows : (g + 1) * rows
            ]
        return 0

    lax.fori_loop(0, kvheads * group // pair, one, 0)


def on_device(n, heads, queries, new_keys, new_values, pool_keys, pool_values, o_weight, page_list):
    rows, qheads, width = queries.shape
    kvheads = new_keys.shape[1]
    group = qheads // kvheads
    slots, page = pool_keys.shape[:2]
    npages = page_list.shape[0]
    kept = min(slots, 2 * npages // n)
    wide = kvheads * width
    sites = n // CORES
    me = lax.axis_index("ctx")
    head = lax.axis_index("head")
    me_ref = me.reshape(1)
    smem = pl.BlockSpec(memory_space=pltpu.SMEM)
    vmem = pl.BlockSpec(memory_space=pltpu.VMEM)
    hbm = pl.BlockSpec(memory_space=pl.ANY)

    half = rows + kept * page
    payload = pl.pallas_call(
        functools.partial(pack_kernel, slots),
        out_shape=jax.ShapeDtypeStruct((2 * half, wide), jnp.bfloat16),
        in_specs=[smem, smem, vmem, vmem, vmem, vmem],
        out_specs=vmem,
        name="pack_pages",
    )(
        page_list,
        me_ref,
        new_keys.reshape(rows, wide),
        new_values.reshape(rows, wide),
        pool_keys.reshape(slots, page, wide),
        pool_values.reshape(slots, page, wide),
    )
    w_other = core_swap(o_weight, n)
    gathered = ring_gather(payload, sites)
    operands, spots = [], []
    for d in range(sites):
        for swap in range(CORES):
            pieces = gathered[d]
            if swap:
                pieces = [core_swap(p, n) for p in pieces]
            base = len(operands)
            operands += pieces
            spots.append((base, 0, base, half) if len(pieces) == 1 else (base, 0, base + 1, 0))

    total_keys = npages * page + n * rows
    key_block = math.gcd(total_keys, 512)
    cfg = (n, rows, kvheads, group, width, page, slots, kept, key_block)

    def attend(pages_ref, me_ref, q_ref, *refs):
        ins = [(refs[a], b, refs[c], e) for a, b, c, e in spots]
        attend_kernel(cfg, pages_ref, me_ref, q_ref, *ins, *refs[len(operands) :])

    attended = pl.pallas_call(
        attend,
        out_shape=jax.ShapeDtypeStruct((rows, qheads * width), jnp.bfloat16),
        in_specs=[smem, smem, vmem] + [hbm] * len(operands),
        out_specs=vmem,
        scratch_shapes=[
            pltpu.VMEM((total_keys, wide), jnp.bfloat16),
            pltpu.VMEM((total_keys, wide), jnp.bfloat16),
            pltpu.SMEM((n * kept,), jnp.int32),
            pltpu.SMEM((n,), jnp.int32),
            pltpu.SemaphoreType.DMA,
        ],
        compiler_params=pltpu.CompilerParams(vmem_limit_bytes=VMEM_LIMIT),
        cost_estimate=pl.CostEstimate(
            flops=4 * rows * qheads * width * total_keys,
            bytes_accessed=8 * total_keys * wide,
            transcendentals=rows * qheads * total_keys,
        ),
        name="attend",
    )(page_list, me_ref, queries.reshape(rows, qheads * width), *operands)

    blocks = ring_gather(attended, sites)
    cols = o_weight.shape[1]
    place = place_of(me // CORES, sites)

    def product(pieces):
        parts = []
        for w in (o_weight, w_other):
            out = [jnp.dot(p, w, preferred_element_type=jnp.float32) for p in pieces]
            parts.append(out[0] if len(out) == 1 else jnp.concatenate(out, axis=0))
        return parts

    part_rows = rows // heads
    summed = {}
    for d in range(sites):
        own, other = product(blocks[d])
        full = jnp.concatenate([own, other], axis=1)
        mine = lax.dynamic_slice_in_dim(full, head * part_rows, part_rows, 0)
        sent = full.astype(jnp.bfloat16)
        if heads == 2:
            away = lax.dynamic_slice_in_dim(sent, (1 - head) * part_rows, part_rows, 0)
            got = lax.ppermute(away, "head", [(0, 1), (1, 0)])
            summed[d] = (mine + got.astype(jnp.float32)).astype(jnp.bfloat16)
        else:
            summed[d] = lax.psum_scatter(sent, "head", scatter_dimension=0, tiled=True)

    returned = []
    for d in range(sites):
        back = summed[d]
        if d:
            back = lax.ppermute(back, "ctx", site_perm(sites, -d))
        returned.append(back)
    stack = jnp.stack(returned, axis=0)
    order = jnp.stack([jnp.mod(place_of(jnp.int32(s), sites) - place, sites) for s in range(sites)])
    stack = jnp.take(stack, order, axis=0)
    stack = stack.reshape(sites, part_rows, CORES, cols)
    stack = jnp.where(me % CORES == 0, stack, stack[:, :, ::-1])
    stack = stack.transpose(1, 0, 2, 3).reshape(part_rows, sites * CORES * cols)
    return lax.all_to_all(stack, "head", split_axis=1, concat_axis=0, tiled=True)


def solution(mesh):
    n, heads = mesh.shape["ctx"], mesh.shape["head"]
    in_specs = (
        P("ctx", "head", None),
        P("ctx", "head", None),
        P("ctx", "head", None),
        P("ctx", None, "head", None),
        P("ctx", None, "head", None),
        P("head", "ctx"),
        P(),
    )
    out_specs = P("ctx", "head")
    return jax.shard_map(
        functools.partial(on_device, n, heads),
        mesh=mesh,
        in_specs=in_specs,
        out_specs=out_specs,
        check_vma=False,
    )
```

```python
import functools
import math

import jax
import jax.numpy as jnp
from jax import lax
from jax.experimental import pallas as pl
from jax.experimental.pallas import tpu as pltpu
from jax.sharding import PartitionSpec as P

CORES = 2
LINES = 2
NEG = -1e30
VMEM_LIMIT = 32 * 1024 * 1024
FREE = pl.CostEstimate(flops=0, bytes_accessed=0, transcendentals=0)


def cycle_of(sites):
    length = sites // LINES
    order = []
    for line in range(LINES):
        steps = range(length) if line % 2 == 0 else range(length - 1, -1, -1)
        order += [z * LINES + line for z in steps]
    return order


def place_of(site, sites):
    z, line = site // LINES, site % LINES
    length = sites // LINES
    return jnp.where(line == 0, z, 2 * length - 1 - z)


def site_perm(sites, shift):
    order = cycle_of(sites)
    return [
        (order[i] * CORES + k, order[(i + shift) % sites] * CORES + k)
        for i in range(sites)
        for k in range(CORES)
    ]


def core_swap(x, count):
    return lax.ppermute(x, "ctx", [(i, i ^ 1) for i in range(count)])


def ring_walk(block, sites, work):
    ahead = site_perm(sites, 1)
    back = site_perm(sites, -1)
    here, done = {0: [block]}, None
    f = b = block
    steps = sites // 2
    for step in range(1, steps + 1):
        if step < steps or sites % 2:
            f = lax.ppermute(f, "ctx", ahead)
            b = lax.ppermute(b, "ctx", back)
            arrived = {step: [f], sites - step: [b]}
        else:
            half = block.shape[0] // 2
            f = lax.ppermute(f[:half], "ctx", ahead)
            b = lax.ppermute(b[half:], "ctx", back)
            arrived = {step: [f, b]}
        done = work(step - 1, here, done)
        f, b, done = lax.optimization_barrier((f, b, done))
        here = {d: [f, b] if len(p) == 2 else [f] if d == step else [b] for d, p in arrived.items()}
    return work(steps, here, done)


def pack_kernel(slots, pages_ref, me_ref, nk_ref, nv_ref, pk_ref, pv_ref, out_ref):
    rows = nk_ref.shape[0]
    page = pk_ref.shape[1]
    kept = (out_ref.shape[0] // 2 - rows) // page
    half = out_ref.shape[0] // 2
    out_ref[...] = jnp.zeros_like(out_ref)
    out_ref[0:rows, :] = nk_ref[...]
    out_ref[half : half + rows, :] = nv_ref[...]
    me = me_ref[0]

    def one(p, count):
        slot = pages_ref[p]
        mine = slot // slots == me

        @pl.when(jnp.logical_and(mine, count < kept))
        def _():
            local = slot % slots
            at = pl.multiple_of(rows + count * page, page)
            out_ref[pl.ds(at, page), :] = pk_ref[local]
            out_ref[pl.ds(pl.multiple_of(half + at, page), page), :] = pv_ref[local]

        return count + mine.astype(jnp.int32)

    lax.fori_loop(0, pages_ref.shape[0], one, jnp.int32(0))


def attend_kernel(cfg, first, last, counts, me_ref, q_ref, own_ref, ins, state, outs, scratch):
    n, rows, kvheads, group, width, page, slots, kept = cfg
    kbuf, vbuf, sbuf, dup, sem = scratch
    sites = n // CORES
    length = sites // LINES
    span = rows + kept * page
    total_keys = kbuf.shape[0]
    me = me_ref[0]
    my_site, my_core = me // CORES, me % CORES
    my_place = jnp.where(my_site % LINES == 0, my_site // LINES, 2 * length - 1 - my_site // LINES)

    pair = math.gcd(group, 4)
    tall = pair * rows
    steps = kvheads * group // pair
    scale = math.log2(math.e) * width ** (-0.5)
    chunk = CORES * span

    copies = [pltpu.make_async_copy(own_ref.at[0:16], dup, sem)]
    for b, (_, _, k_ref, k_at, v_ref, v_at) in enumerate(ins):
        at = pl.ds(b * span, span)
        copies.append(pltpu.make_async_copy(k_ref.at[pl.ds(k_at, span)], kbuf.at[at], sem))
        for h in range(kvheads):
            copies.append(
                pltpu.make_async_copy(
                    v_ref.at[pl.ds(v_at, span), pl.ds(h * width, width)],
                    vbuf.at[at, pl.ds(2 * h * width, width)],
                    sem,
                )
            )
    for copy in copies:
        copy.start()
    for h in range(kvheads):
        vbuf[:, (2 * h + 1) * width : (2 * h + 2) * width] = jnp.ones(
            (total_keys, width), jnp.bfloat16
        )
    for copy in copies:
        copy.wait()

    seen_key = dup[0:1, :]
    for b, (d, swap, *_) in enumerate(ins):
        place = lax.rem(my_place + sites - d, sites)
        line = place // length
        z = jnp.where(line == 0, place, 2 * length - 1 - place)
        owner = (z * LINES + line) * CORES + lax.rem(my_core + swap, CORES)

        def blank(at, size):
            kbuf[at : at + size, :] = jnp.broadcast_to(seen_key, (size, kbuf.shape[1]))
            vbuf[at : at + size, :] = jnp.zeros((size, vbuf.shape[1]), jnp.bfloat16)

        @pl.when(owner > me)
        def _():
            blank(b * span, rows)

        for j in range(kept):

            @pl.when(j >= counts[owner])
            def _():
                blank(b * span + rows + j * page, page)

    def lanes(i):
        return pl.ds(pl.multiple_of(i * width, width), width)

    def scores(i, slot):
        h = i // (group // pair)
        q = jnp.concatenate([q_ref[:, lanes(i * pair + g)] for g in range(pair)], axis=0)
        top = jnp.full((tall, width), NEG, jnp.float32)
        for j in range(total_keys // chunk):
            k = kbuf[j * chunk : (j + 1) * chunk, lanes(h)]
            s = lax.dot_general(q, k, (((1,), (1,)), ((), ())), preferred_element_type=jnp.float32)
            for a in range(chunk // width):
                piece = s[:, a * width : (a + 1) * width]
                at = j * chunk + a * width
                if first and at < rows:
                    row = lax.broadcasted_iota(jnp.int32, (rows, width), 0)
                    col = lax.broadcasted_iota(jnp.int32, (rows, width), 1) + at
                    seen = jnp.concatenate([col <= row] * pair, axis=0)
                    piece = jnp.where(seen, piece, NEG)
                sbuf[slot, :, at : at + width] = piece
                top = jnp.maximum(top, piece)
        return top

    def weigh(i, slot, top):
        h = i // (group // pair)
        at = pl.ds(pl.multiple_of(i * tall, tall), tall)
        best = jnp.max(top, axis=1, keepdims=True)
        if not first:
            was = state[1][at, 0:1]
            best = jnp.maximum(best, was)
        shift = best * scale
        acc = None
        for j in range(total_keys // chunk):
            s = sbuf[slot, :, j * chunk : (j + 1) * chunk]
            w = jnp.exp2(s * scale - shift).astype(jnp.bfloat16)
            v = vbuf[
                j * chunk : (j + 1) * chunk, pl.ds(pl.multiple_of(2 * h * width, width), 2 * width)
            ]
            part = jnp.dot(w, v, preferred_element_type=jnp.float32)
            acc = part if acc is None else acc + part
        mixed, total = acc[:, :width], acc[:, width:]
        if not first:
            left = jnp.exp2(was * scale - shift)
            mixed = mixed + state[0][at, :] * left
            total = total + state[1][at, width // 2 : width // 2 + 1] * left
        if last:
            out = (mixed / total).astype(jnp.bfloat16)
            for g in range(pair):
                outs[0][:, lanes(i * pair + g)] = out[g * rows : (g + 1) * rows]
        else:
            lane = lax.broadcasted_iota(jnp.int32, (tall, width), 1)
            outs[0][at, :] = mixed
            outs[1][at, :] = jnp.where(lane < width // 2, best, total)

    top = scores(0, 0)

    def two(t, top):
        after = scores(2 * t + 1, 1)
        weigh(2 * t, 0, top)
        top = scores(jnp.minimum(2 * t + 2, steps - 1), 0)
        weigh(2 * t + 1, 1, after)
        return top

    lax.fori_loop(0, steps // 2, two, top)


def attend(cfg, live, me_ref, queries, payload, blocks, state, last):
    n, rows, kvheads, group, width, page, slots, kept = cfg
    span = rows + kept * page
    smem = pl.BlockSpec(memory_space=pltpu.SMEM)
    vmem = pl.BlockSpec(memory_space=pltpu.VMEM)
    hbm = pl.BlockSpec(memory_space=pl.ANY)
    operands, spots = [], []
    for d, swap, pieces in blocks:
        base = len(operands)
        operands += pieces
        one = len(pieces) == 1
        spots.append((d, swap, base, 0, base if one else base + 1, span if one else 0))
    first = state is None
    state = [] if first else list(state)
    total_keys = len(blocks) * span
    tall = math.gcd(group, 4) * rows
    qrows = rows * kvheads * group
    if last:
        out_shape = [jax.ShapeDtypeStruct((rows, kvheads * group * width), jnp.bfloat16)]
    else:
        out_shape = [jax.ShapeDtypeStruct((qrows, width), jnp.float32)] * 2

    def body(live_ref, me_ref, q_ref, own_ref, *refs):
        ins = [(d, swap, refs[a], b, refs[c], e) for d, swap, a, b, c, e in spots]
        rest = refs[len(operands) :]
        held, rest = rest[: len(state)], rest[len(state) :]
        outs, scratch = rest[: len(out_shape)], rest[len(out_shape) :]
        attend_kernel(
            cfg, first, last, live_ref, me_ref, q_ref, own_ref, ins, held, outs, scratch
        )

    return pl.pallas_call(
        body,
        out_shape=out_shape,
        in_specs=[smem, smem, vmem, hbm] + [hbm] * len(operands) + [vmem] * len(state),
        out_specs=[vmem] * len(out_shape),
        scratch_shapes=[
            pltpu.VMEM((total_keys, kvheads * width), jnp.bfloat16),
            pltpu.VMEM((total_keys, 2 * kvheads * width), jnp.bfloat16),
            pltpu.VMEM((2, tall, total_keys), jnp.float32),
            pltpu.VMEM((16, kvheads * width), jnp.bfloat16),
            pltpu.SemaphoreType.DMA,
        ],
        compiler_params=pltpu.CompilerParams(vmem_limit_bytes=VMEM_LIMIT),
        cost_estimate=pl.CostEstimate(
            flops=4 * qrows * width * total_keys, bytes_accessed=0, transcendentals=0
        ),
        name="attend_last" if last else "attend",
    )(live, me_ref, queries, payload, *operands, *state)


def product(spots, pieces, own, other, split):
    depth, cols = own.shape
    tile = min(256, cols)
    half = cols // tile
    rows = sum(p.shape[0] for p in pieces)
    heads, blocks = (split, len(pieces)) if split else (1, 1)
    part = rows // blocks // heads
    assert heads <= 2

    def body(spots_ref, *refs):
        a_refs, rest = refs[: len(pieces)], refs[len(pieces) :]
        own_ref, other_ref, *outs = rest

        def run(w_ref):
            a = jnp.concatenate([r[...] for r in a_refs], axis=0)
            out = jnp.dot(a, w_ref[...], preferred_element_type=jnp.float32)
            if not split:
                outs[0][...] = out.astype(jnp.bfloat16)
                return
            keep_ref, sent_ref, acc = outs
            acc[...] = out
            head = spots_ref[1]
            for b in range(blocks):
                keep_ref[b * part : (b + 1) * part, :] = acc[
                    pl.ds(pl.multiple_of((b * heads + head) * part, part), part), :
                ]
                sent_ref[b * part : (b + 1) * part, :] = acc[
                    pl.ds(pl.multiple_of((b * heads + 1 - head) * part, part), part), :
                ].astype(jnp.bfloat16)

        t = pl.program_id(0)
        pl.when(t < half)(lambda: run(own_ref))
        pl.when(t >= half)(lambda: run(other_ref))

    out_spec = pl.BlockSpec(
        (rows // heads, tile), lambda t, s: (0, lax.rem(t + half * s[0], 2 * half))
    )
    shape = (rows // heads, 2 * cols)
    outs = [jax.ShapeDtypeStruct(shape, jnp.bfloat16)]
    if split:
        outs = [jax.ShapeDtypeStruct(shape, jnp.float32)] + outs
    return pl.pallas_call(
        body,
        out_shape=outs,
        grid_spec=pltpu.PrefetchScalarGridSpec(
            num_scalar_prefetch=1,
            grid=(2 * half,),
            in_specs=[pl.BlockSpec(p.shape, lambda t, s: (0, 0)) for p in pieces]
            + [
                pl.BlockSpec((depth, tile), lambda t, s: (0, jnp.minimum(t, half - 1))),
                pl.BlockSpec((depth, tile), lambda t, s: (0, jnp.maximum(t - half, 0))),
            ],
            out_specs=[out_spec] * len(outs),
            scratch_shapes=[pltpu.VMEM((rows, tile), jnp.float32)] if split else [],
        ),
        compiler_params=pltpu.CompilerParams(vmem_limit_bytes=VMEM_LIMIT),
        cost_estimate=pl.CostEstimate(
            flops=4 * rows * depth * cols, bytes_accessed=0, transcendentals=0
        ),
        name="product",
    )(spots, *pieces, own, other)


def back_perms(sites, heads, shift):
    order = cycle_of(sites)
    within, across = [], []
    for i in range(sites):
        source, target = order[i], order[(i - shift) % sites]
        goal = source * heads // sites
        for k in range(CORES):
            for h in range(heads):
                pair = ((source * CORES + k) * heads + h, (target * CORES + k) * heads + goal)
                (within if h == goal else across).append(pair)
    return within, across


def assemble_kernel(sites, heads, spots_ref, *refs):
    ins, (out_ref, left, right, sem) = refs[:-4], refs[-4:]
    length = sites // LINES
    cols = out_ref.shape[1] * heads // sites
    rows = out_ref.shape[0]
    part = rows // heads
    place, head = spots_ref[2], spots_ref[1]

    def each(go):
        for d in range(sites):
            at = lax.rem(place + d, sites)
            line = at // length
            z = jnp.where(line == 0, at, 2 * length - 1 - at)
            site = z * LINES + line
            first, second = ins[2 * d], ins[2 * d + 1]

            @pl.when(site * heads // sites == head)
            def _():
                lane = pl.multiple_of((site - head * (sites // heads)) * cols, cols)
                if first.shape[0] == rows:
                    slot = 0 if d == 0 else 1
                    if go is None:
                        total = left[slot].astype(jnp.float32) + right[slot].astype(jnp.float32)
                        out_ref[:, pl.ds(lane, cols)] = total.astype(jnp.bfloat16)
                        return
                    a = pltpu.make_async_copy(first, left.at[slot], sem)
                    b = pltpu.make_async_copy(second, right.at[slot], sem)
                elif go is None:
                    return
                else:
                    mine = pl.multiple_of(head * part, part)
                    other = pl.multiple_of((1 - head) * part, part)
                    a = pltpu.make_async_copy(
                        first, out_ref.at[pl.ds(mine, part), pl.ds(lane, cols)], sem
                    )
                    b = pltpu.make_async_copy(
                        second, out_ref.at[pl.ds(other, part), pl.ds(lane, cols)], sem
                    )
                go(a)
                go(b)

    each(lambda c: c.start())
    each(lambda c: c.wait())
    each(None)


def on_device(n, heads, queries, new_keys, new_values, pool_keys, pool_values, o_weight, page_list):
    rows, qheads, width = queries.shape
    kvheads = new_keys.shape[1]
    group = qheads // kvheads
    slots, page = pool_keys.shape[:2]
    npages = page_list.shape[0]
    kept = min(slots, 2 * npages // n)
    wide = kvheads * width
    sites = n // CORES
    cols = o_weight.shape[1]
    me = lax.axis_index("ctx")
    head = lax.axis_index("head")
    me_ref = me.reshape(1)
    place = place_of(me // CORES, sites)
    spots = jnp.stack([me % CORES, head, place]).astype(jnp.int32)
    smem = pl.BlockSpec(memory_space=pltpu.SMEM)
    vmem = pl.BlockSpec(memory_space=pltpu.VMEM)
    hbm = pl.BlockSpec(memory_space=pl.ANY)

    half = rows + kept * page
    payload = pl.pallas_call(
        functools.partial(pack_kernel, slots),
        out_shape=jax.ShapeDtypeStruct((2 * half, wide), jnp.bfloat16),
        in_specs=[smem, smem, vmem, vmem, vmem, vmem],
        out_specs=vmem,
        cost_estimate=FREE,
        name="pack_pages",
    )(
        page_list,
        me_ref,
        new_keys.reshape(rows, wide),
        new_values.reshape(rows, wide),
        pool_keys.reshape(slots, page, wide),
        pool_values.reshape(slots, page, wide),
    )
    w_other = core_swap(o_weight, n)
    q = queries.reshape(rows, qheads * width)
    cfg = (n, rows, kvheads, group, width, page, slots, kept)
    live = jnp.sum(
        (page_list // slots)[None, :] == jnp.arange(n, dtype=jnp.int32)[:, None], axis=1
    ).astype(jnp.int32)

    def look(step, here, state):
        blocks = []
        for d, pieces in here.items():
            blocks.append((d, 0, pieces))
            blocks.append((d, 1, [core_swap(p, n) for p in pieces]))
        return attend(cfg, live, me_ref, q, payload, blocks, state, step == sites // 2)

    (attended,) = ring_walk(payload, sites, look)

    if heads != 2 or sites % 2:
        parts = {}

        def multiply(step, here, _):
            for d, pieces in here.items():
                (part,) = product(spots, pieces, o_weight, w_other, 0)
                parts[d] = lax.ppermute(part, "ctx", site_perm(sites, -d)) if d else part
            return part

        ring_walk(attended, sites, multiply)
        order = jnp.stack(
            [jnp.mod(place_of(jnp.int32(s), sites) - place, sites) for s in range(sites)]
        )
        full = jnp.take(jnp.stack([parts[d] for d in range(sites)], axis=0), order, axis=0)
        full = full.transpose(1, 0, 2).reshape(rows, sites * CORES * cols)
        return lax.psum_scatter(full, "head", scatter_dimension=1, tiled=True)

    both = ("ctx", "head")
    arrived = {}

    def multiply(step, here, _):
        if step in (0, sites // 2):
            (part,) = product(spots, here[step], o_weight, w_other, 0)
            within, across = back_perms(sites, heads, step)
            first = lax.ppermute(part, both, within) if step else part
            arrived[step] = [first, lax.ppermute(part, both, across)]
            return part
        d, e = step, sites - step
        keep, sent = product(spots, here[d] + here[e], o_weight, w_other, heads)
        got = lax.ppermute(sent, "head", [(0, 1), (1, 0)])
        total = (keep + got.astype(jnp.float32)).astype(jnp.bfloat16)
        part = total.shape[0] // 2
        for at, piece in ((d, total[:part]), (e, total[part:])):
            arrived[at] = [
                lax.ppermute(piece, both, perm) for perm in back_perms(sites, heads, at)
            ]
        return sent

    ring_walk(attended, sites, multiply)
    return pl.pallas_call(
        functools.partial(assemble_kernel, sites, heads),
        out_shape=jax.ShapeDtypeStruct((rows, sites * CORES * cols // heads), jnp.bfloat16),
        in_specs=[smem] + [hbm] * (2 * sites),
        out_specs=vmem,
        scratch_shapes=[
            pltpu.VMEM((2, rows, CORES * cols), jnp.bfloat16),
            pltpu.VMEM((2, rows, CORES * cols), jnp.bfloat16),
            pltpu.SemaphoreType.DMA,
        ],
        cost_estimate=FREE,
        name="assemble",
    )(spots, *[a for d in range(sites) for a in arrived[d]])


def solution(mesh):
    n, heads = mesh.shape["ctx"], mesh.shape["head"]
    in_specs = (
        P("ctx", "head", None),
        P("ctx", "head", None),
        P("ctx", "head", None),
        P("ctx", None, "head", None),
        P("ctx", None, "head", None),
        P("head", "ctx"),
        P(),
    )
    out_specs = P("ctx", "head")
    return jax.shard_map(
        functools.partial(on_device, n, heads),
        mesh=mesh,
        in_specs=in_specs,
        out_specs=out_specs,
        check_vma=False,
    )
```

```python
import functools
import math

import jax
import jax.numpy as jnp
from jax import lax
from jax.experimental import pallas as pl
from jax.experimental.pallas import tpu as pltpu
from jax.sharding import PartitionSpec as P

CORES = 2
LINES = 2
NEG = -1e30
VMEM_LIMIT = 32 * 1024 * 1024
FREE = pl.CostEstimate(flops=0, bytes_accessed=0, transcendentals=0)


def cycle_of(sites):
    length = sites // LINES
    order = []
    for line in range(LINES):
        steps = range(length) if line % 2 == 0 else range(length - 1, -1, -1)
        order += [z * LINES + line for z in steps]
    return order


def place_of(site, sites):
    z, line = site // LINES, site % LINES
    length = sites // LINES
    return jnp.where(line == 0, z, 2 * length - 1 - z)


def site_perm(sites, shift):
    order = cycle_of(sites)
    return [
        (order[i] * CORES + k, order[(i + shift) % sites] * CORES + k)
        for i in range(sites)
        for k in range(CORES)
    ]


def core_swap(x, count):
    return lax.ppermute(x, "ctx", [(i, i ^ 1) for i in range(count)])


def ring_walk(block, sites, work):
    ahead = site_perm(sites, 1)
    back = site_perm(sites, -1)
    here, done, late = {0: [block]}, None, []
    f = b = block
    steps = sites // 2
    for step in range(1, steps + 1):
        if step < steps or sites % 2:
            f = lax.ppermute(f, "ctx", ahead)
            b = lax.ppermute(b, "ctx", back)
            arrived = {step: [f], sites - step: [b]}
        else:
            half = block.shape[0] // 2
            f = lax.ppermute(f[:half], "ctx", ahead)
            b = lax.ppermute(b[half:], "ctx", back)
            arrived = {step: [f, b]}
        done, later = work(step - 1, here, done)
        f, b, done, _ = lax.optimization_barrier((f, b, done, late))
        late = later
        here = {d: [f, b] if len(p) == 2 else [f] if d == step else [b] for d, p in arrived.items()}
    return work(steps, here, done)[0]


def pack_kernel(slots, pages_ref, me_ref, nk_ref, nv_ref, pk_ref, pv_ref, out_ref):
    rows = nk_ref.shape[0]
    page = pk_ref.shape[1]
    kept = (out_ref.shape[0] // 2 - rows) // page
    half = out_ref.shape[0] // 2
    out_ref[...] = jnp.zeros_like(out_ref)
    heads, width = nk_ref.shape[1:]
    for h in range(heads):
        lanes = slice(h * width, (h + 1) * width)
        out_ref[0:rows, lanes] = nk_ref[:, h, :]
        out_ref[half : half + rows, lanes] = nv_ref[:, h, :]
    me = me_ref[0]

    def one(p, count):
        slot = pages_ref[p]
        mine = slot // slots == me

        @pl.when(jnp.logical_and(mine, count < kept))
        def _():
            local = slot % slots
            at = pl.multiple_of(rows + count * page, page)
            for h in range(heads):
                lanes = slice(h * width, (h + 1) * width)
                out_ref[pl.ds(at, page), lanes] = pk_ref[local, :, h, :]
                out_ref[pl.ds(pl.multiple_of(half + at, page), page), lanes] = pv_ref[
                    local, :, h, :
                ]

        return count + mine.astype(jnp.int32)

    lax.fori_loop(0, pages_ref.shape[0], one, jnp.int32(0))


def attend_kernel(cfg, first, last, counts, me_ref, q_ref, own_ref, ins, state, outs, scratch):
    n, rows, kvheads, group, width, page, slots, kept = cfg
    kbuf, vbuf, sbuf, dup, sem = scratch
    sites = n // CORES
    length = sites // LINES
    span = rows + kept * page
    total_keys = kbuf.shape[0]
    me = me_ref[0]
    my_site, my_core = me // CORES, me % CORES
    my_place = jnp.where(my_site % LINES == 0, my_site // LINES, 2 * length - 1 - my_site // LINES)

    pair = math.gcd(group, 4)
    tall = pair * rows
    steps = kvheads * group // pair
    scale = math.log2(math.e) * width ** (-0.5)
    chunk = CORES * span

    copies = [pltpu.make_async_copy(own_ref.at[0:16], dup, sem)]
    for b, (_, _, k_ref, k_at, v_ref, v_at) in enumerate(ins):
        at = pl.ds(b * span, span)
        copies.append(pltpu.make_async_copy(k_ref.at[pl.ds(k_at, span)], kbuf.at[at], sem))
        for h in range(kvheads):
            copies.append(
                pltpu.make_async_copy(
                    v_ref.at[pl.ds(v_at, span), pl.ds(h * width, width)],
                    vbuf.at[at, pl.ds(2 * h * width, width)],
                    sem,
                )
            )
    for copy in copies:
        copy.start()
    for h in range(kvheads):
        vbuf[:, (2 * h + 1) * width : (2 * h + 2) * width] = jnp.ones(
            (total_keys, width), jnp.bfloat16
        )
    for copy in copies:
        copy.wait()

    seen_key = dup[0:1, :]
    for b, (d, swap, *_) in enumerate(ins):
        place = lax.rem(my_place + sites - d, sites)
        line = place // length
        z = jnp.where(line == 0, place, 2 * length - 1 - place)
        owner = (z * LINES + line) * CORES + lax.rem(my_core + swap, CORES)

        def blank(at, size):
            kbuf[at : at + size, :] = jnp.broadcast_to(seen_key, (size, kbuf.shape[1]))
            vbuf[at : at + size, :] = jnp.zeros((size, vbuf.shape[1]), jnp.bfloat16)

        @pl.when(owner > me)
        def _():
            blank(b * span, rows)

        for j in range(kept):

            @pl.when(j >= counts[owner])
            def _():
                blank(b * span + rows + j * page, page)

    def lanes(i):
        return pl.ds(pl.multiple_of(i * width, width), width)

    def scores(i, slot):
        h = i // (group // pair)
        q = jnp.concatenate([q_ref[:, lanes(i * pair + g)] for g in range(pair)], axis=0)
        top = jnp.full((tall, width), NEG, jnp.float32)
        for j in range(total_keys // chunk):
            k = kbuf[j * chunk : (j + 1) * chunk, lanes(h)]
            s = lax.dot_general(q, k, (((1,), (1,)), ((), ())), preferred_element_type=jnp.float32)
            for a in range(chunk // width):
                piece = s[:, a * width : (a + 1) * width]
                at = j * chunk + a * width
                if first and at < rows:
                    row = lax.broadcasted_iota(jnp.int32, (rows, width), 0)
                    col = lax.broadcasted_iota(jnp.int32, (rows, width), 1) + at
                    seen = jnp.concatenate([col <= row] * pair, axis=0)
                    piece = jnp.where(seen, piece, NEG)
                sbuf[slot, :, at : at + width] = piece
                top = jnp.maximum(top, piece)
        return top

    def weigh(i, slot, top):
        h = i // (group // pair)
        at = pl.ds(pl.multiple_of(i * tall, tall), tall)
        best = jnp.max(top, axis=1, keepdims=True)
        if not first:
            was = state[1][at, 0:1]
            best = jnp.maximum(best, was)
        shift = best * scale
        acc = None
        for j in range(total_keys // chunk):
            s = sbuf[slot, :, j * chunk : (j + 1) * chunk]
            w = jnp.exp2(s * scale - shift).astype(jnp.bfloat16)
            v = vbuf[
                j * chunk : (j + 1) * chunk, pl.ds(pl.multiple_of(2 * h * width, width), 2 * width)
            ]
            part = jnp.dot(w, v, preferred_element_type=jnp.float32)
            acc = part if acc is None else acc + part
        mixed, total = acc[:, :width], acc[:, width:]
        if not first:
            left = jnp.exp2(was * scale - shift)
            mixed = mixed + state[0][at, :] * left
            total = total + state[1][at, width // 2 : width // 2 + 1] * left
        if last:
            out = (mixed / total).astype(jnp.bfloat16)
            for g in range(pair):
                outs[0][:, lanes(i * pair + g)] = out[g * rows : (g + 1) * rows]
        else:
            lane = lax.broadcasted_iota(jnp.int32, (tall, width), 1)
            outs[0][at, :] = mixed
            outs[1][at, :] = jnp.where(lane < width // 2, best, total)

    top = scores(0, 0)

    def two(t, top):
        after = scores(2 * t + 1, 1)
        weigh(2 * t, 0, top)
        top = scores(jnp.minimum(2 * t + 2, steps - 1), 0)
        weigh(2 * t + 1, 1, after)
        return top

    lax.fori_loop(0, steps // 2, two, top)


def attend(cfg, live, me_ref, queries, payload, blocks, state, last):
    n, rows, kvheads, group, width, page, slots, kept = cfg
    span = rows + kept * page
    smem = pl.BlockSpec(memory_space=pltpu.SMEM)
    vmem = pl.BlockSpec(memory_space=pltpu.VMEM)
    hbm = pl.BlockSpec(memory_space=pl.ANY)
    operands, spots = [], []
    for d, swap, pieces in blocks:
        base = len(operands)
        operands += pieces
        one = len(pieces) == 1
        spots.append((d, swap, base, 0, base if one else base + 1, span if one else 0))
    first = state is None
    state = [] if first else list(state)
    total_keys = len(blocks) * span
    tall = math.gcd(group, 4) * rows
    qrows = rows * kvheads * group
    if last:
        out_shape = [jax.ShapeDtypeStruct((rows, kvheads * group * width), jnp.bfloat16)]
    else:
        out_shape = [jax.ShapeDtypeStruct((qrows, width), jnp.float32)] * 2

    def body(live_ref, me_ref, q_ref, own_ref, *refs):
        ins = [(d, swap, refs[a], b, refs[c], e) for d, swap, a, b, c, e in spots]
        rest = refs[len(operands) :]
        held, rest = rest[: len(state)], rest[len(state) :]
        outs, scratch = rest[: len(out_shape)], rest[len(out_shape) :]
        attend_kernel(
            cfg, first, last, live_ref, me_ref, q_ref, own_ref, ins, held, outs, scratch
        )

    return pl.pallas_call(
        body,
        out_shape=out_shape,
        in_specs=[smem, smem, vmem, hbm] + [hbm] * len(operands) + [vmem] * len(state),
        out_specs=[vmem] * len(out_shape),
        scratch_shapes=[
            pltpu.VMEM((total_keys, kvheads * width), jnp.bfloat16),
            pltpu.VMEM((total_keys, 2 * kvheads * width), jnp.bfloat16),
            pltpu.VMEM((2, tall, total_keys), jnp.float32),
            pltpu.VMEM((16, kvheads * width), jnp.bfloat16),
            pltpu.SemaphoreType.DMA,
        ],
        compiler_params=pltpu.CompilerParams(vmem_limit_bytes=VMEM_LIMIT),
        cost_estimate=pl.CostEstimate(
            flops=4 * qrows * width * total_keys, bytes_accessed=0, transcendentals=0
        ),
        name="attend_last" if last else "attend",
    )(live, me_ref, queries, payload, *operands, *state)


def product(spots, pieces, own, other, split):
    depth, cols = own.shape
    tile = min(256, cols)
    half = cols // tile
    rows = sum(p.shape[0] for p in pieces)
    heads, blocks = (split, len(pieces)) if split else (1, 1)
    part = rows // blocks // heads
    assert heads <= 2

    def body(spots_ref, *refs):
        a_refs, rest = refs[: len(pieces)], refs[len(pieces) :]
        own_ref, other_ref, *outs = rest

        def run(w_ref):
            a = jnp.concatenate([r[...] for r in a_refs], axis=0)
            out = jnp.dot(a, w_ref[...], preferred_element_type=jnp.float32)
            if not split:
                outs[0][...] = out.astype(jnp.bfloat16)
                return
            keep_ref, sent_ref, acc = outs
            acc[...] = out
            head = spots_ref[1]
            for b in range(blocks):
                keep_ref[b * part : (b + 1) * part, :] = acc[
                    pl.ds(pl.multiple_of((b * heads + head) * part, part), part), :
                ]
                sent_ref[b * part : (b + 1) * part, :] = acc[
                    pl.ds(pl.multiple_of((b * heads + 1 - head) * part, part), part), :
                ].astype(jnp.bfloat16)

        t = pl.program_id(0)
        pl.when(t < half)(lambda: run(own_ref))
        pl.when(t >= half)(lambda: run(other_ref))

    out_spec = pl.BlockSpec(
        (rows // heads, tile), lambda t, s: (0, lax.rem(t + half * s[0], 2 * half))
    )
    shape = (rows // heads, 2 * cols)
    outs = [jax.ShapeDtypeStruct(shape, jnp.bfloat16)]
    if split:
        outs = [jax.ShapeDtypeStruct(shape, jnp.float32)] + outs
    return pl.pallas_call(
        body,
        out_shape=outs,
        grid_spec=pltpu.PrefetchScalarGridSpec(
            num_scalar_prefetch=1,
            grid=(2 * half,),
            in_specs=[pl.BlockSpec(p.shape, lambda t, s: (0, 0)) for p in pieces]
            + [
                pl.BlockSpec((depth, tile), lambda t, s: (0, jnp.minimum(t, half - 1))),
                pl.BlockSpec((depth, tile), lambda t, s: (0, jnp.maximum(t - half, 0))),
            ],
            out_specs=[out_spec] * len(outs),
            scratch_shapes=[pltpu.VMEM((rows, tile), jnp.float32)] if split else [],
        ),
        compiler_params=pltpu.CompilerParams(vmem_limit_bytes=VMEM_LIMIT),
        cost_estimate=pl.CostEstimate(
            flops=4 * rows * depth * cols, bytes_accessed=0, transcendentals=0
        ),
        name="product",
    )(spots, *pieces, own, other)


def back_perms(sites, heads, shift):
    order = cycle_of(sites)
    within, across = [], []
    for i in range(sites):
        source, target = order[i], order[(i - shift) % sites]
        goal = source * heads // sites
        for k in range(CORES):
            for h in range(heads):
                pair = ((source * CORES + k) * heads + h, (target * CORES + k) * heads + goal)
                (within if h == goal else across).append(pair)
    return within, across


def assemble_kernel(sites, heads, spans, spots_ref, *refs):
    ins, (out_ref, left, right, sem) = refs[:-4], refs[-4:]
    length = sites // LINES
    cols = out_ref.shape[1] * heads // sites
    rows = out_ref.shape[0]
    part = rows // heads
    place, head = spots_ref[2], spots_ref[1]

    def each(go):
        for d in range(sites):
            at = lax.rem(place + d, sites)
            line = at // length
            z = jnp.where(line == 0, at, 2 * length - 1 - at)
            site = z * LINES + line
            size = rows if d in (0, sites // 2) else part
            first, second = [ins[i].at[pl.ds(off, size)] for i, off in spans[d]]

            @pl.when(site * heads // sites == head)
            def _():
                lane = pl.multiple_of((site - head * (sites // heads)) * cols, cols)
                if size == rows:
                    slot = 0 if d == 0 else 1
                    if go is None:
                        total = left[slot].astype(jnp.float32) + right[slot].astype(jnp.float32)
                        out_ref[:, pl.ds(lane, cols)] = total.astype(jnp.bfloat16)
                        return
                    a = pltpu.make_async_copy(first, left.at[slot], sem)
                    b = pltpu.make_async_copy(second, right.at[slot], sem)
                elif go is None:
                    return
                else:
                    mine = pl.multiple_of(head * part, part)
                    other = pl.multiple_of((1 - head) * part, part)
                    a = pltpu.make_async_copy(
                        first, out_ref.at[pl.ds(mine, part), pl.ds(lane, cols)], sem
                    )
                    b = pltpu.make_async_copy(
                        second, out_ref.at[pl.ds(other, part), pl.ds(lane, cols)], sem
                    )
                go(a)
                go(b)

    each(lambda c: c.start())
    each(lambda c: c.wait())
    each(None)


def on_device(n, heads, queries, new_keys, new_values, pool_keys, pool_values, o_weight, page_list):
    rows, qheads, width = queries.shape
    kvheads = new_keys.shape[1]
    group = qheads // kvheads
    slots, page = pool_keys.shape[:2]
    npages = page_list.shape[0]
    kept = min(slots, 2 * npages // n)
    wide = kvheads * width
    sites = n // CORES
    cols = o_weight.shape[1]
    me = lax.axis_index("ctx")
    head = lax.axis_index("head")
    me_ref = me.reshape(1)
    place = place_of(me // CORES, sites)
    spots = jnp.stack([me % CORES, head, place]).astype(jnp.int32)
    smem = pl.BlockSpec(memory_space=pltpu.SMEM)
    vmem = pl.BlockSpec(memory_space=pltpu.VMEM)
    hbm = pl.BlockSpec(memory_space=pl.ANY)

    half = rows + kept * page
    payload = pl.pallas_call(
        functools.partial(pack_kernel, slots),
        out_shape=jax.ShapeDtypeStruct((2 * half, wide), jnp.bfloat16),
        in_specs=[smem, smem, vmem, vmem, vmem, vmem],
        out_specs=vmem,
        cost_estimate=FREE,
        name="pack_pages",
    )(
        page_list,
        me_ref,
        new_keys,
        new_values,
        pool_keys,
        pool_values,
    )
    w_other = core_swap(o_weight, n)
    q = queries.reshape(rows, qheads * width)
    cfg = (n, rows, kvheads, group, width, page, slots, kept)
    live = jnp.sum(
        (page_list // slots)[None, :] == jnp.arange(n, dtype=jnp.int32)[:, None], axis=1
    ).astype(jnp.int32)

    def look(step, here, state):
        blocks = []
        for d, pieces in here.items():
            blocks.append((d, 0, pieces))
            blocks.append((d, 1, [core_swap(p, n) for p in pieces]))
        return attend(cfg, live, me_ref, q, payload, blocks, state, step == sites // 2), []

    (attended,) = ring_walk(payload, sites, look)

    if heads != 2 or sites % 2:
        parts = {}

        def multiply(step, here, _):
            for d, pieces in here.items():
                (part,) = product(spots, pieces, o_weight, w_other, 0)
                parts[d] = lax.ppermute(part, "ctx", site_perm(sites, -d)) if d else part
            return part, []

        ring_walk(attended, sites, multiply)
        order = jnp.stack(
            [jnp.mod(place_of(jnp.int32(s), sites) - place, sites) for s in range(sites)]
        )
        full = jnp.take(jnp.stack([parts[d] for d in range(sites)], axis=0), order, axis=0)
        full = full.transpose(1, 0, 2).reshape(rows, sites * CORES * cols)
        return lax.psum_scatter(full, "head", scatter_dimension=1, tiled=True)

    both = ("ctx", "head")
    arrived = {}

    last = sites // 2
    summing, crossing = [], []

    def swap_heads(x):
        return lax.ppermute(x, "head", [(0, 1), (1, 0)])

    def halves(d, keep, got):
        total = (keep + got.astype(jnp.float32)).astype(jnp.bfloat16)
        half = total.shape[0] // 2
        return total, ((d, total[:half]), (sites - d, total[half:]))

    def cross():
        for d, first, second in crossing:
            got = swap_heads(jnp.concatenate([first, second], axis=0))
            half = first.shape[0]
            arrived[d], arrived[sites - d] = [(first, 0), (got, 0)], [(second, 0), (got, half)]
            crossing.clear()
            return [got]
        return []

    def multiply(step, here, _):
        if step in (0, last):
            (part,) = product(spots, here[step], o_weight, w_other, 0)
            if summing:
                d, keep, got = summing
                keep, got, part = lax.optimization_barrier((keep, got, part))
            within, across = back_perms(sites, heads, step)
            first = lax.ppermute(part, both, within) if step else part
            arrived[step] = [(first, 0), (lax.ppermute(part, both, across), 0)]
            cross()
            if summing:
                for at, piece in halves(d, keep, got)[1]:
                    arrived[at] = [
                        (lax.ppermute(piece, both, perm), 0)
                        for perm in back_perms(sites, heads, at)
                    ]
            return [part], [arrived[step][1][0]]
        keep, sent = product(spots, here[step] + here[sites - step], o_weight, w_other, heads)
        got = swap_heads(sent)
        crossed = cross()
        if step == last - 1:
            summing.extend((step, keep, got))
            return [sent], crossed
        total, pieces = halves(step, keep, got)
        back = [lax.ppermute(p, "ctx", site_perm(sites, -at)) for at, p in pieces]
        crossing.append((step, *back))
        return [total], back + crossed

    ring_walk(attended, sites, multiply)
    operands, spans = [], []
    for d in range(sites):
        spans.append([(len(operands) + i, off) for i, (_, off) in enumerate(arrived[d])])
        operands += [x for x, _ in arrived[d]]
    return pl.pallas_call(
        functools.partial(assemble_kernel, sites, heads, spans),
        out_shape=jax.ShapeDtypeStruct((rows, sites * CORES * cols // heads), jnp.bfloat16),
        in_specs=[smem] + [hbm] * len(operands),
        out_specs=vmem,
        scratch_shapes=[
            pltpu.VMEM((2, rows, CORES * cols), jnp.bfloat16),
            pltpu.VMEM((2, rows, CORES * cols), jnp.bfloat16),
            pltpu.SemaphoreType.DMA,
        ],
        cost_estimate=FREE,
        name="assemble",
    )(spots, *operands)


def solution(mesh):
    n, heads = mesh.shape["ctx"], mesh.shape["head"]
    in_specs = (
        P("ctx", "head", None),
        P("ctx", "head", None),
        P("ctx", "head", None),
        P("ctx", None, "head", None),
        P("ctx", None, "head", None),
        P("head", "ctx"),
        P(),
    )
    out_specs = P("ctx", "head")
    return jax.shard_map(
        functools.partial(on_device, n, heads),
        mesh=mesh,
        in_specs=in_specs,
        out_specs=out_specs,
        check_vma=False,
    )
```

```python
import functools
import math

import jax
import jax.numpy as jnp
from jax import lax
from jax.experimental import pallas as pl
from jax.experimental.pallas import tpu as pltpu
from jax.sharding import PartitionSpec as P

CORES = 2
LINES = 2
NEG = -1e30
VMEM_LIMIT = 24 * 1024 * 1024
SMALL_LIMIT = 12 * 1024 * 1024
FREE = pl.CostEstimate(flops=0, bytes_accessed=0, transcendentals=0)


def cycle_of(sites):
    length = sites // LINES
    order = []
    for line in range(LINES):
        steps = range(length) if line % 2 == 0 else range(length - 1, -1, -1)
        order += [z * LINES + line for z in steps]
    return order


def place_of(site, sites):
    z, line = site // LINES, site % LINES
    length = sites // LINES
    return jnp.where(line == 0, z, 2 * length - 1 - z)


def site_perm(sites, shift):
    order = cycle_of(sites)
    return [
        (order[i] * CORES + k, order[(i + shift) % sites] * CORES + k)
        for i in range(sites)
        for k in range(CORES)
    ]


def core_swap(x, count):
    return lax.ppermute(x, "ctx", [(i, i ^ 1) for i in range(count)])


def ring_walk(block, sites, work):
    steps = sites // 2
    here, done = {0: [block]}, None
    f = b = block
    for step in range(1, steps + 1):
        if step < steps or sites % 2:
            f = lax.ppermute(f, "ctx", site_perm(sites, 1))
            b = lax.ppermute(b, "ctx", site_perm(sites, -1))
            arrived = {step: [f], sites - step: [b]}
        else:
            half = block.shape[0] // 2
            f = lax.ppermute(f[:half], "ctx", site_perm(sites, 1))
            b = lax.ppermute(b[half:], "ctx", site_perm(sites, -1))
            arrived = {step: [f, b]}
        done = work(step - 1, here, done)
        f, b, done = lax.optimization_barrier((f, b, done))
        here = {d: [f, b] if len(p) == 2 else [f] if d == step else [b] for d, p in arrived.items()}
    return work(steps, here, done)


def pack_kernel(slots, pages_ref, me_ref, nk_ref, nv_ref, pk_ref, pv_ref, out_ref):
    rows = nk_ref.shape[0]
    page = pk_ref.shape[1]
    kept = (out_ref.shape[0] // 2 - rows) // page
    half = out_ref.shape[0] // 2
    out_ref[...] = jnp.zeros_like(out_ref)
    heads, width = nk_ref.shape[1:]
    for h in range(heads):
        lanes = slice(h * width, (h + 1) * width)
        out_ref[0:rows, lanes] = nk_ref[:, h, :]
        out_ref[half : half + rows, lanes] = nv_ref[:, h, :]
    me = me_ref[0]

    def one(p, count):
        slot = pages_ref[p]
        mine = slot // slots == me

        @pl.when(jnp.logical_and(mine, count < kept))
        def _():
            local = slot % slots
            at = pl.multiple_of(rows + count * page, page)
            for h in range(heads):
                lanes = slice(h * width, (h + 1) * width)
                out_ref[pl.ds(at, page), lanes] = pk_ref[local, :, h, :]
                out_ref[pl.ds(pl.multiple_of(half + at, page), page), lanes] = pv_ref[
                    local, :, h, :
                ]

        return count + mine.astype(jnp.int32)

    lax.fori_loop(0, pages_ref.shape[0], one, jnp.int32(0))


def attend_kernel(cfg, first, last, counts, me_ref, q_ref, own_ref, ins, state, outs, scratch):
    n, rows, kvheads, group, width, page, slots, kept = cfg
    kbuf, vbuf, sbuf, dup, sem = scratch
    sites = n // CORES
    length = sites // LINES
    span = rows + kept * page
    total_keys = kbuf.shape[0]
    me = me_ref[0]
    my_site, my_core = me // CORES, me % CORES
    my_place = jnp.where(my_site % LINES == 0, my_site // LINES, 2 * length - 1 - my_site // LINES)

    pair = math.gcd(group, 4)
    tall = pair * rows
    steps = kvheads * group // pair
    scale = math.log2(math.e) * width ** (-0.5)
    chunk = CORES * span

    copies = [pltpu.make_async_copy(own_ref.at[0:16], dup, sem)]
    for b, (_, _, k_ref, k_at, v_ref, v_at) in enumerate(ins):
        at = pl.ds(b * span, span)
        copies.append(pltpu.make_async_copy(k_ref.at[pl.ds(k_at, span)], kbuf.at[at], sem))
        for h in range(kvheads):
            copies.append(
                pltpu.make_async_copy(
                    v_ref.at[pl.ds(v_at, span), pl.ds(h * width, width)],
                    vbuf.at[at, pl.ds(2 * h * width, width)],
                    sem,
                )
            )
    for copy in copies:
        copy.start()
    for h in range(kvheads):
        vbuf[:, (2 * h + 1) * width : (2 * h + 2) * width] = jnp.ones(
            (total_keys, width), jnp.bfloat16
        )
    for copy in copies:
        copy.wait()

    seen_key = dup[0:1, :]
    for b, (d, swap, *_) in enumerate(ins):
        place = lax.rem(my_place + sites - d, sites)
        line = place // length
        z = jnp.where(line == 0, place, 2 * length - 1 - place)
        owner = (z * LINES + line) * CORES + lax.rem(my_core + swap, CORES)

        def blank(at, size):
            kbuf[at : at + size, :] = jnp.broadcast_to(seen_key, (size, kbuf.shape[1]))
            vbuf[at : at + size, :] = jnp.zeros((size, vbuf.shape[1]), jnp.bfloat16)

        @pl.when(owner > me)
        def _():
            blank(b * span, rows)

        for j in range(kept):

            @pl.when(j >= counts[owner])
            def _():
                blank(b * span + rows + j * page, page)

    def lanes(i):
        return pl.ds(pl.multiple_of(i * width, width), width)

    def scores(i, slot):
        h = i // (group // pair)
        q = jnp.concatenate([q_ref[:, lanes(i * pair + g)] for g in range(pair)], axis=0)
        top = jnp.full((tall, width), NEG, jnp.float32)
        for j in range(total_keys // chunk):
            k = kbuf[j * chunk : (j + 1) * chunk, lanes(h)]
            s = lax.dot_general(q, k, (((1,), (1,)), ((), ())), preferred_element_type=jnp.float32)
            for a in range(chunk // width):
                piece = s[:, a * width : (a + 1) * width]
                at = j * chunk + a * width
                if first and at < rows:
                    row = lax.broadcasted_iota(jnp.int32, (rows, width), 0)
                    col = lax.broadcasted_iota(jnp.int32, (rows, width), 1) + at
                    seen = jnp.concatenate([col <= row] * pair, axis=0)
                    piece = jnp.where(seen, piece, NEG)
                sbuf[slot, :, at : at + width] = piece
                top = jnp.maximum(top, piece)
        return top

    def weigh(i, slot, top):
        h = i // (group // pair)
        at = pl.ds(pl.multiple_of(i * tall, tall), tall)
        best = jnp.max(top, axis=1, keepdims=True)
        if not first:
            was = state[1][at, 0:1]
            best = jnp.maximum(best, was)
        shift = best * scale
        acc = None
        for j in range(total_keys // chunk):
            s = sbuf[slot, :, j * chunk : (j + 1) * chunk]
            w = jnp.exp2(s * scale - shift).astype(jnp.bfloat16)
            v = vbuf[
                j * chunk : (j + 1) * chunk, pl.ds(pl.multiple_of(2 * h * width, width), 2 * width)
            ]
            part = jnp.dot(w, v, preferred_element_type=jnp.float32)
            acc = part if acc is None else acc + part
        mixed, total = acc[:, :width], acc[:, width:]
        if not first:
            left = jnp.exp2(was * scale - shift)
            mixed = mixed + state[0][at, :] * left
            total = total + state[1][at, width // 2 : width // 2 + 1] * left
        if last:
            out = (mixed / total).astype(jnp.bfloat16)
            for g in range(pair):
                outs[0][:, lanes(i * pair + g)] = out[g * rows : (g + 1) * rows]
        else:
            lane = lax.broadcasted_iota(jnp.int32, (tall, width), 1)
            outs[0][at, :] = mixed
            outs[1][at, :] = jnp.where(lane < width // 2, best, total)

    top = scores(0, 0)

    def two(t, top):
        after = scores(2 * t + 1, 1)
        weigh(2 * t, 0, top)
        top = scores(jnp.minimum(2 * t + 2, steps - 1), 0)
        weigh(2 * t + 1, 1, after)
        return top

    lax.fori_loop(0, steps // 2, two, top)


def attend(cfg, live, me_ref, queries, payload, blocks, state, last):
    n, rows, kvheads, group, width, page, slots, kept = cfg
    span = rows + kept * page
    smem = pl.BlockSpec(memory_space=pltpu.SMEM)
    vmem = pl.BlockSpec(memory_space=pltpu.VMEM)
    hbm = pl.BlockSpec(memory_space=pl.ANY)
    operands, spots = [], []
    for d, swap, pieces in blocks:
        base = len(operands)
        operands += pieces
        one = len(pieces) == 1
        spots.append((d, swap, base, 0, base if one else base + 1, span if one else 0))
    first = state is None
    state = [] if first else list(state)
    total_keys = len(blocks) * span
    tall = math.gcd(group, 4) * rows
    qrows = rows * kvheads * group
    if last:
        out_shape = [jax.ShapeDtypeStruct((rows, kvheads * group * width), jnp.bfloat16)]
    else:
        out_shape = [jax.ShapeDtypeStruct((qrows, width), jnp.float32)] * 2

    def body(live_ref, me_ref, q_ref, own_ref, *refs):
        ins = [(d, swap, refs[a], b, refs[c], e) for d, swap, a, b, c, e in spots]
        rest = refs[len(operands) :]
        held, rest = rest[: len(state)], rest[len(state) :]
        outs, scratch = rest[: len(out_shape)], rest[len(out_shape) :]
        attend_kernel(
            cfg, first, last, live_ref, me_ref, q_ref, own_ref, ins, held, outs, scratch
        )

    return pl.pallas_call(
        body,
        out_shape=out_shape,
        in_specs=[smem, smem, vmem, hbm] + [hbm] * len(operands) + [vmem] * len(state),
        out_specs=[vmem] * len(out_shape),
        scratch_shapes=[
            pltpu.VMEM((total_keys, kvheads * width), jnp.bfloat16),
            pltpu.VMEM((total_keys, 2 * kvheads * width), jnp.bfloat16),
            pltpu.VMEM((2, tall, total_keys), jnp.float32),
            pltpu.VMEM((16, kvheads * width), jnp.bfloat16),
            pltpu.SemaphoreType.DMA,
        ],
        compiler_params=pltpu.CompilerParams(vmem_limit_bytes=VMEM_LIMIT),
        cost_estimate=pl.CostEstimate(
            flops=4 * qrows * width * total_keys, bytes_accessed=0, transcendentals=0
        ),
        name="attend_last" if last else "attend",
    )(live, me_ref, queries, payload, *operands, *state)


def product(spots, pieces, own, other, split):
    depth, cols = own.shape
    tile = min(256, cols)
    half = cols // tile
    rows = sum(p.shape[0] for p in pieces)
    heads, blocks = (split, len(pieces)) if split else (1, 1)
    part = rows // blocks // heads
    assert heads <= 2

    def body(spots_ref, *refs):
        a_refs, rest = refs[: len(pieces)], refs[len(pieces) :]
        own_ref, other_ref, *outs = rest
        core, head = spots_ref[0], spots_ref[1]
        a = jnp.concatenate([r[...] for r in a_refs], axis=0)
        for t in range(2 * half):
            w_ref = own_ref if t < half else other_ref
            at = pl.multiple_of(lax.rem(t + half * core, 2 * half) * tile, tile)
            lanes = pl.ds(at, tile)
            columns = slice((t % half) * tile, (t % half + 1) * tile)
            out = jnp.dot(a, w_ref[:, columns], preferred_element_type=jnp.float32)
            if not split:
                outs[0][:, lanes] = out.astype(jnp.bfloat16)
                continue
            keep_ref, sent_ref, acc = outs
            acc[...] = out
            for b in range(blocks):
                mine = pl.ds(pl.multiple_of((b * heads + head) * part, part), part)
                rest = pl.ds(pl.multiple_of((b * heads + 1 - head) * part, part), part)
                keep_ref[b * part : (b + 1) * part, lanes] = acc[mine, :]
                sent_ref[b * part : (b + 1) * part, lanes] = acc[rest, :].astype(jnp.bfloat16)

    shape = (rows // heads, 2 * cols)
    outs = [jax.ShapeDtypeStruct(shape, jnp.bfloat16)]
    if split:
        outs = [jax.ShapeDtypeStruct(shape, jnp.float32)] + outs
    vmem = pl.BlockSpec(memory_space=pltpu.VMEM)
    return pl.pallas_call(
        body,
        out_shape=outs,
        in_specs=[pl.BlockSpec(memory_space=pltpu.SMEM)] + [vmem] * (len(pieces) + 2),
        out_specs=[vmem] * len(outs),
        scratch_shapes=[pltpu.VMEM((rows, tile), jnp.float32)] if split else [],
        compiler_params=pltpu.CompilerParams(vmem_limit_bytes=VMEM_LIMIT),
        cost_estimate=pl.CostEstimate(
            flops=4 * rows * depth * cols, bytes_accessed=0, transcendentals=0
        ),
        name="product",
    )(spots, *pieces, own, other)


def back_perms(sites, heads, shift):
    order = cycle_of(sites)
    within, across = [], []
    for i in range(sites):
        source, target = order[i], order[(i - shift) % sites]
        goal = source * heads // sites
        for k in range(CORES):
            for h in range(heads):
                pair = ((source * CORES + k) * heads + h, (target * CORES + k) * heads + goal)
                (within if h == goal else across).append(pair)
    return within, across


def assemble_kernel(sites, heads, spans, spots_ref, *refs):
    ins, out_ref = refs[:-1], refs[-1]
    length = sites // LINES
    rows = out_ref.shape[0]
    cols = out_ref.shape[1] * heads // sites
    part = rows // heads
    place, head = spots_ref[2], spots_ref[1]
    for d in range(sites):
        at = lax.rem(place + d, sites)
        line = at // length
        z = jnp.where(line == 0, at, 2 * length - 1 - at)
        site = z * LINES + line
        (first, first_at), (second, second_at) = [(ins[i], off) for i, off in spans[d]]

        @pl.when(site * heads // sites == head)
        def _():
            lanes = pl.ds(pl.multiple_of((site - head * (sites // heads)) * cols, cols), cols)
            if d in (0, sites // 2):
                total = first[...].astype(jnp.float32) + second[...].astype(jnp.float32)
                out_ref[:, lanes] = total.astype(jnp.bfloat16)
            else:
                mine = pl.ds(pl.multiple_of(head * part, part), part)
                other = pl.ds(pl.multiple_of((1 - head) * part, part), part)
                out_ref[mine, lanes] = first[first_at : first_at + part, :]
                out_ref[other, lanes] = second[second_at : second_at + part, :]


def on_device(n, heads, queries, new_keys, new_values, pool_keys, pool_values, o_weight, page_list):
    rows, qheads, width = queries.shape
    kvheads = new_keys.shape[1]
    group = qheads // kvheads
    slots, page = pool_keys.shape[:2]
    npages = page_list.shape[0]
    kept = min(slots, 2 * npages // n)
    wide = kvheads * width
    sites = n // CORES
    cols = o_weight.shape[1]
    me = lax.axis_index("ctx")
    head = lax.axis_index("head")
    me_ref = me.reshape(1)
    place = place_of(me // CORES, sites)
    spots = jnp.stack([me % CORES, head, place]).astype(jnp.int32)
    smem = pl.BlockSpec(memory_space=pltpu.SMEM)
    vmem = pl.BlockSpec(memory_space=pltpu.VMEM)
    hbm = pl.BlockSpec(memory_space=pl.ANY)

    half = rows + kept * page
    payload = pl.pallas_call(
        functools.partial(pack_kernel, slots),
        out_shape=jax.ShapeDtypeStruct((2 * half, wide), jnp.bfloat16),
        in_specs=[smem, smem, vmem, vmem, vmem, vmem],
        out_specs=vmem,
        cost_estimate=FREE,
        name="pack_pages",
    )(
        page_list,
        me_ref,
        new_keys,
        new_values,
        pool_keys,
        pool_values,
    )
    w_other = core_swap(o_weight, n)
    q = queries.reshape(rows, qheads * width)
    cfg = (n, rows, kvheads, group, width, page, slots, kept)
    live = jnp.sum(
        (page_list // slots)[None, :] == jnp.arange(n, dtype=jnp.int32)[:, None], axis=1
    ).astype(jnp.int32)

    def look(step, here, state):
        blocks = []
        for d, pieces in here.items():
            blocks.append((d, 0, pieces))
            blocks.append((d, 1, [core_swap(p, n) for p in pieces]))
        return attend(cfg, live, me_ref, q, payload, blocks, state, step == sites // 2)

    (attended,) = ring_walk(payload, sites, look)

    if heads != 2 or sites % 2:
        parts = {}

        def multiply(step, here, _):
            for d, pieces in here.items():
                (part,) = product(spots, pieces, o_weight, w_other, 0)
                parts[d] = lax.ppermute(part, "ctx", site_perm(sites, -d)) if d else part
            return part

        ring_walk(attended, sites, multiply)
        order = jnp.stack(
            [jnp.mod(place_of(jnp.int32(s), sites) - place, sites) for s in range(sites)]
        )
        full = jnp.take(jnp.stack([parts[d] for d in range(sites)], axis=0), order, axis=0)
        full = full.transpose(1, 0, 2).reshape(rows, sites * CORES * cols)
        return lax.psum_scatter(full, "head", scatter_dimension=1, tiled=True)

    both = ("ctx", "head")
    arrived = {}

    last = sites // 2
    summing, crossing = [], []

    def swap_heads(x):
        return lax.ppermute(x, "head", [(0, 1), (1, 0)])

    def halves(d, keep, got):
        total = (keep + got.astype(jnp.float32)).astype(jnp.bfloat16)
        half = total.shape[0] // 2
        return total, ((d, total[:half]), (sites - d, total[half:]))

    def cross(after=()):
        for d, first, second in crossing:
            first, second, _ = lax.optimization_barrier((first, second, after))
            got = swap_heads(jnp.concatenate([first, second], axis=0))
            half = first.shape[0]
            arrived[d], arrived[sites - d] = [(first, 0), (got, 0)], [(second, 0), (got, half)]
            crossing.clear()
            return [got]
        return []

    def multiply(step, here, _):
        if step in (0, last):
            (part,) = product(spots, here[step], o_weight, w_other, 0)
            if summing:
                d, keep, got = summing
                keep, got, part = lax.optimization_barrier((keep, got, part))
            within, across = back_perms(sites, heads, step)
            first = lax.ppermute(part, both, within) if step else part
            arrived[step] = [(first, 0), (lax.ppermute(part, both, across), 0)]
            cross(part)
            if summing:
                for at, piece in halves(d, keep, got)[1]:
                    arrived[at] = [
                        (lax.ppermute(piece, both, perm), 0)
                        for perm in back_perms(sites, heads, at)
                    ]
            return [part, arrived[0][1][0]] if step == 0 else [part]
        keep, sent = product(spots, here[step] + here[sites - step], o_weight, w_other, heads)
        got = swap_heads(sent)
        cross()
        if step == last - 1:
            summing.extend((step, keep, got))
            return [sent]
        total, pieces = halves(step, keep, got)
        back = [lax.ppermute(p, "ctx", site_perm(sites, -at)) for at, p in pieces]
        crossing.append((step, *back))
        return [total]

    ring_walk(attended, sites, multiply)
    operands, spans = [], []
    for d in range(sites):
        spans.append([(len(operands) + i, off) for i, (_, off) in enumerate(arrived[d])])
        operands += [x for x, _ in arrived[d]]
    return pl.pallas_call(
        functools.partial(assemble_kernel, sites, heads, spans),
        out_shape=jax.ShapeDtypeStruct((rows, sites * CORES * cols // heads), jnp.bfloat16),
        in_specs=[smem] + [vmem] * len(operands),
        out_specs=vmem,
        compiler_params=pltpu.CompilerParams(vmem_limit_bytes=SMALL_LIMIT),
        cost_estimate=FREE,
        name="assemble",
    )(spots, *operands)


def solution(mesh):
    n, heads = mesh.shape["ctx"], mesh.shape["head"]
    in_specs = (
        P("ctx", "head", None),
        P("ctx", "head", None),
        P("ctx", "head", None),
        P("ctx", None, "head", None),
        P("ctx", None, "head", None),
        P("head", "ctx"),
        P(),
    )
    out_specs = P("ctx", "head")
    return jax.shard_map(
        functools.partial(on_device, n, heads),
        mesh=mesh,
        in_specs=in_specs,
        out_specs=out_specs,
        check_vma=False,
    )
```

```python
import functools
import math

import jax
import jax.numpy as jnp
from jax import lax
from jax.experimental import pallas as pl
from jax.experimental.pallas import tpu as pltpu
from jax.sharding import PartitionSpec as P

CORES = 2
LINES = 2
NEG = -1e30
VMEM_LIMIT = 24 * 1024 * 1024
SMALL_LIMIT = 12 * 1024 * 1024
FREE = pl.CostEstimate(flops=0, bytes_accessed=0, transcendentals=0)


def cycle_of(sites):
    length = sites // LINES
    order = []
    for line in range(LINES):
        steps = range(length) if line % 2 == 0 else range(length - 1, -1, -1)
        order += [z * LINES + line for z in steps]
    return order


def place_of(site, sites):
    z, line = site // LINES, site % LINES
    length = sites // LINES
    return jnp.where(line == 0, z, 2 * length - 1 - z)


def site_perm(sites, shift):
    order = cycle_of(sites)
    return [
        (order[i] * CORES + k, order[(i + shift) % sites] * CORES + k)
        for i in range(sites)
        for k in range(CORES)
    ]


def core_swap(x, count):
    return lax.ppermute(x, "ctx", [(i, i ^ 1) for i in range(count)])


def ring_walk(block, sites, work):
    steps = sites // 2
    here, done = {0: [block]}, None
    f = b = block
    for step in range(1, steps + 1):
        if step < steps or sites % 2:
            f = lax.ppermute(f, "ctx", site_perm(sites, 1))
            b = lax.ppermute(b, "ctx", site_perm(sites, -1))
            arrived = {step: [f], sites - step: [b]}
        else:
            half = block.shape[0] // 2
            f = lax.ppermute(f[:half], "ctx", site_perm(sites, 1))
            b = lax.ppermute(b[half:], "ctx", site_perm(sites, -1))
            arrived = {step: [f, b]}
        done = work(step - 1, here, done)
        f, b, done = lax.optimization_barrier((f, b, done))
        here = {d: [f, b] if len(p) == 2 else [f] if d == step else [b] for d, p in arrived.items()}
    return work(steps, here, done)


def pack_kernel(slots, pages_ref, me_ref, nk_ref, nv_ref, pk_ref, pv_ref, out_ref):
    rows = nk_ref.shape[0]
    page = pk_ref.shape[1]
    kept = (out_ref.shape[0] // 2 - rows) // page
    half = out_ref.shape[0] // 2
    out_ref[...] = jnp.zeros_like(out_ref)
    heads, width = nk_ref.shape[1:]
    for h in range(heads):
        lanes = slice(h * width, (h + 1) * width)
        out_ref[0:rows, lanes] = nk_ref[:, h, :]
        out_ref[half : half + rows, lanes] = nv_ref[:, h, :]
    me = me_ref[0]

    def one(p, count):
        slot = pages_ref[p]
        mine = slot // slots == me

        @pl.when(jnp.logical_and(mine, count < kept))
        def _():
            local = slot % slots
            at = pl.multiple_of(rows + count * page, page)
            for h in range(heads):
                lanes = slice(h * width, (h + 1) * width)
                out_ref[pl.ds(at, page), lanes] = pk_ref[local, :, h, :]
                out_ref[pl.ds(pl.multiple_of(half + at, page), page), lanes] = pv_ref[
                    local, :, h, :
                ]

        return count + mine.astype(jnp.int32)

    lax.fori_loop(0, pages_ref.shape[0], one, jnp.int32(0))


def attend_kernel(cfg, first, last, counts, me_ref, q_ref, own_ref, ins, state, outs, scratch):
    n, rows, kvheads, group, width, page, slots, kept = cfg
    kbuf, vbuf, sbuf, dup, sem = scratch
    sites = n // CORES
    length = sites // LINES
    span = rows + kept * page
    total_keys = kbuf.shape[0]
    me = me_ref[0]
    my_site, my_core = me // CORES, me % CORES
    my_place = jnp.where(my_site % LINES == 0, my_site // LINES, 2 * length - 1 - my_site // LINES)

    pair = math.gcd(group, 4)
    tall = pair * rows
    steps = kvheads * group // pair
    scale = math.log2(math.e) * width ** (-0.5)
    chunk = CORES * span

    copies = [pltpu.make_async_copy(own_ref.at[0:16], dup, sem)]
    for b, (_, _, k_ref, k_at, v_ref, v_at) in enumerate(ins):
        at = pl.ds(b * span, span)
        copies.append(pltpu.make_async_copy(k_ref.at[pl.ds(k_at, span)], kbuf.at[at], sem))
        for h in range(kvheads):
            copies.append(
                pltpu.make_async_copy(
                    v_ref.at[pl.ds(v_at, span), pl.ds(h * width, width)],
                    vbuf.at[at, pl.ds(2 * h * width, width)],
                    sem,
                )
            )
    for copy in copies:
        copy.start()
    for h in range(kvheads):
        vbuf[:, (2 * h + 1) * width : (2 * h + 2) * width] = jnp.ones(
            (total_keys, width), jnp.bfloat16
        )
    for copy in copies:
        copy.wait()

    seen_key = dup[0:1, :]
    for b, (d, swap, *_) in enumerate(ins):
        place = lax.rem(my_place + sites - d, sites)
        line = place // length
        z = jnp.where(line == 0, place, 2 * length - 1 - place)
        owner = (z * LINES + line) * CORES + lax.rem(my_core + swap, CORES)

        def blank(at, size):
            kbuf[at : at + size, :] = jnp.broadcast_to(seen_key, (size, kbuf.shape[1]))
            vbuf[at : at + size, :] = jnp.zeros((size, vbuf.shape[1]), jnp.bfloat16)

        @pl.when(owner > me)
        def _():
            blank(b * span, rows)

        for j in range(kept):

            @pl.when(j >= counts[owner])
            def _():
                blank(b * span + rows + j * page, page)

    def lanes(i):
        return pl.ds(pl.multiple_of(i * width, width), width)

    def scores(i, slot):
        h = i // (group // pair)
        q = jnp.concatenate([q_ref[:, lanes(i * pair + g)] for g in range(pair)], axis=0)
        top = jnp.full((tall, width), NEG, jnp.float32)
        for j in range(total_keys // chunk):
            k = kbuf[j * chunk : (j + 1) * chunk, lanes(h)]
            s = lax.dot_general(q, k, (((1,), (1,)), ((), ())), preferred_element_type=jnp.float32)
            for a in range(chunk // width):
                piece = s[:, a * width : (a + 1) * width]
                at = j * chunk + a * width
                if first and at < rows:
                    row = lax.broadcasted_iota(jnp.int32, (rows, width), 0)
                    col = lax.broadcasted_iota(jnp.int32, (rows, width), 1) + at
                    seen = jnp.concatenate([col <= row] * pair, axis=0)
                    piece = jnp.where(seen, piece, NEG)
                sbuf[slot, :, at : at + width] = piece
                top = jnp.maximum(top, piece)
        return top

    def weigh(i, slot, top):
        h = i // (group // pair)
        at = pl.ds(pl.multiple_of(i * tall, tall), tall)
        best = jnp.max(top, axis=1, keepdims=True)
        if not first:
            was = state[1][at, 0:1]
            best = jnp.maximum(best, was)
        shift = best * scale
        acc = None
        for j in range(total_keys // chunk):
            s = sbuf[slot, :, j * chunk : (j + 1) * chunk]
            w = jnp.exp2(s * scale - shift).astype(jnp.bfloat16)
            v = vbuf[
                j * chunk : (j + 1) * chunk, pl.ds(pl.multiple_of(2 * h * width, width), 2 * width)
            ]
            part = jnp.dot(w, v, preferred_element_type=jnp.float32)
            acc = part if acc is None else acc + part
        mixed, total = acc[:, :width], acc[:, width:]
        if not first:
            left = jnp.exp2(was * scale - shift)
            mixed = mixed + state[0][at, :] * left
            total = total + state[1][at, width // 2 : width // 2 + 1] * left
        if last:
            out = (mixed / total).astype(jnp.bfloat16)
            for g in range(pair):
                outs[0][:, lanes(i * pair + g)] = out[g * rows : (g + 1) * rows]
        else:
            lane = lax.broadcasted_iota(jnp.int32, (tall, width), 1)
            outs[0][at, :] = mixed
            outs[1][at, :] = jnp.where(lane < width // 2, best, total)

    top = scores(0, 0)

    def two(t, top):
        after = scores(2 * t + 1, 1)
        weigh(2 * t, 0, top)
        top = scores(jnp.minimum(2 * t + 2, steps - 1), 0)
        weigh(2 * t + 1, 1, after)
        return top

    lax.fori_loop(0, steps // 2, two, top)


def attend(cfg, live, me_ref, queries, payload, blocks, state, last):
    n, rows, kvheads, group, width, page, slots, kept = cfg
    span = rows + kept * page
    smem = pl.BlockSpec(memory_space=pltpu.SMEM)
    vmem = pl.BlockSpec(memory_space=pltpu.VMEM)
    hbm = pl.BlockSpec(memory_space=pl.ANY)
    operands, spots = [], []
    for d, swap, pieces in blocks:
        base = len(operands)
        operands += pieces
        one = len(pieces) == 1
        spots.append((d, swap, base, 0, base if one else base + 1, span if one else 0))
    first = state is None
    state = [] if first else list(state)
    total_keys = len(blocks) * span
    tall = math.gcd(group, 4) * rows
    qrows = rows * kvheads * group
    if last:
        out_shape = [jax.ShapeDtypeStruct((rows, kvheads * group * width), jnp.bfloat16)]
    else:
        out_shape = [jax.ShapeDtypeStruct((qrows, width), jnp.float32)] * 2

    def body(live_ref, me_ref, q_ref, own_ref, *refs):
        ins = [(d, swap, refs[a], b, refs[c], e) for d, swap, a, b, c, e in spots]
        rest = refs[len(operands) :]
        held, rest = rest[: len(state)], rest[len(state) :]
        outs, scratch = rest[: len(out_shape)], rest[len(out_shape) :]
        attend_kernel(
            cfg, first, last, live_ref, me_ref, q_ref, own_ref, ins, held, outs, scratch
        )

    return pl.pallas_call(
        body,
        out_shape=out_shape,
        in_specs=[smem, smem, vmem, hbm] + [hbm] * len(operands) + [vmem] * len(state),
        out_specs=[vmem] * len(out_shape),
        scratch_shapes=[
            pltpu.VMEM((total_keys, kvheads * width), jnp.bfloat16),
            pltpu.VMEM((total_keys, 2 * kvheads * width), jnp.bfloat16),
            pltpu.VMEM((2, tall, total_keys), jnp.float32),
            pltpu.VMEM((16, kvheads * width), jnp.bfloat16),
            pltpu.SemaphoreType.DMA,
        ],
        compiler_params=pltpu.CompilerParams(vmem_limit_bytes=VMEM_LIMIT),
        cost_estimate=pl.CostEstimate(
            flops=4 * qrows * width * total_keys, bytes_accessed=0, transcendentals=0
        ),
        name="attend_last" if last else "attend",
    )(live, me_ref, queries, payload, *operands, *state)


def product(spots, pieces, own, other, split):
    depth, cols = own.shape
    tile = min(256, cols)
    half = cols // tile
    rows = sum(p.shape[0] for p in pieces)
    heads, blocks = (split, len(pieces)) if split else (1, 1)
    part = rows // blocks // heads
    assert heads <= 2

    def body(spots_ref, *refs):
        a_refs, rest = refs[: len(pieces)], refs[len(pieces) :]
        own_ref, other_ref, *outs = rest
        core, head = spots_ref[0], spots_ref[1]
        a = jnp.concatenate([r[...] for r in a_refs], axis=0)
        for t in range(2 * half):
            w_ref = own_ref if t < half else other_ref
            at = pl.multiple_of(lax.rem(t + half * core, 2 * half) * tile, tile)
            lanes = pl.ds(at, tile)
            columns = slice((t % half) * tile, (t % half + 1) * tile)
            out = jnp.dot(a, w_ref[:, columns], preferred_element_type=jnp.float32)
            if not split:
                outs[0][:, lanes] = out.astype(jnp.bfloat16)
                continue
            keep_ref, sent_ref, acc = outs
            acc[...] = out
            for b in range(blocks):
                mine = pl.ds(pl.multiple_of((b * heads + head) * part, part), part)
                rest = pl.ds(pl.multiple_of((b * heads + 1 - head) * part, part), part)
                keep_ref[b * part : (b + 1) * part, lanes] = acc[mine, :]
                sent_ref[b * part : (b + 1) * part, lanes] = acc[rest, :].astype(jnp.bfloat16)

    shape = (rows // heads, 2 * cols)
    outs = [jax.ShapeDtypeStruct(shape, jnp.bfloat16)]
    if split:
        outs = [jax.ShapeDtypeStruct(shape, jnp.float32)] + outs
    vmem = pl.BlockSpec(memory_space=pltpu.VMEM)
    return pl.pallas_call(
        body,
        out_shape=outs,
        in_specs=[pl.BlockSpec(memory_space=pltpu.SMEM)] + [vmem] * (len(pieces) + 2),
        out_specs=[vmem] * len(outs),
        scratch_shapes=[pltpu.VMEM((rows, tile), jnp.float32)] if split else [],
        compiler_params=pltpu.CompilerParams(vmem_limit_bytes=VMEM_LIMIT),
        cost_estimate=pl.CostEstimate(
            flops=4 * rows * depth * cols, bytes_accessed=0, transcendentals=0
        ),
        name="product",
    )(spots, *pieces, own, other)


def back_perms(sites, heads, shift):
    order = cycle_of(sites)
    within, across = [], []
    for i in range(sites):
        source, target = order[i], order[(i - shift) % sites]
        goal = source * heads // sites
        for k in range(CORES):
            for h in range(heads):
                pair = ((source * CORES + k) * heads + h, (target * CORES + k) * heads + goal)
                (within if h == goal else across).append(pair)
    return within, across


def assemble_kernel(sites, heads, spans, spots_ref, *refs):
    ins, out_ref = refs[:-1], refs[-1]
    length = sites // LINES
    rows = out_ref.shape[0]
    cols = out_ref.shape[1] * heads // sites
    part = rows // heads
    place, head = spots_ref[2], spots_ref[1]
    for d in range(sites):
        at = lax.rem(place + d, sites)
        line = at // length
        z = jnp.where(line == 0, at, 2 * length - 1 - at)
        site = z * LINES + line
        (first, first_at), (second, second_at) = [(ins[i], off) for i, off in spans[d]]

        @pl.when(site * heads // sites == head)
        def _():
            lanes = pl.ds(pl.multiple_of((site - head * (sites // heads)) * cols, cols), cols)
            if d in (0, sites // 2):
                total = first[...].astype(jnp.float32) + second[...].astype(jnp.float32)
                out_ref[:, lanes] = total.astype(jnp.bfloat16)
            else:
                mine = pl.ds(pl.multiple_of(head * part, part), part)
                other = pl.ds(pl.multiple_of((1 - head) * part, part), part)
                out_ref[mine, lanes] = first[first_at : first_at + part, :]
                out_ref[other, lanes] = second[second_at : second_at + part, :]


def join_kernel(count, *refs):
    refs[-1][...] = jnp.concatenate([r[...] for r in refs[:count]], axis=0)


def join(pieces, after):
    vmem = pl.BlockSpec(memory_space=pltpu.VMEM)
    rows = sum(p.shape[0] for p in pieces)
    return pl.pallas_call(
        functools.partial(join_kernel, len(pieces)),
        out_shape=jax.ShapeDtypeStruct((rows, pieces[0].shape[1]), pieces[0].dtype),
        in_specs=[vmem] * len(pieces) + [pl.BlockSpec(memory_space=pl.ANY)],
        out_specs=vmem,
        compiler_params=pltpu.CompilerParams(vmem_limit_bytes=SMALL_LIMIT),
        cost_estimate=FREE,
        name="join",
    )(*pieces, after)


def on_device(n, heads, queries, new_keys, new_values, pool_keys, pool_values, o_weight, page_list):
    rows, qheads, width = queries.shape
    kvheads = new_keys.shape[1]
    group = qheads // kvheads
    slots, page = pool_keys.shape[:2]
    npages = page_list.shape[0]
    kept = min(slots, 2 * npages // n)
    wide = kvheads * width
    sites = n // CORES
    cols = o_weight.shape[1]
    me = lax.axis_index("ctx")
    head = lax.axis_index("head")
    me_ref = me.reshape(1)
    place = place_of(me // CORES, sites)
    spots = jnp.stack([me % CORES, head, place]).astype(jnp.int32)
    smem = pl.BlockSpec(memory_space=pltpu.SMEM)
    vmem = pl.BlockSpec(memory_space=pltpu.VMEM)
    hbm = pl.BlockSpec(memory_space=pl.ANY)

    half = rows + kept * page
    payload = pl.pallas_call(
        functools.partial(pack_kernel, slots),
        out_shape=jax.ShapeDtypeStruct((2 * half, wide), jnp.bfloat16),
        in_specs=[smem, smem, vmem, vmem, vmem, vmem],
        out_specs=vmem,
        cost_estimate=FREE,
        name="pack_pages",
    )(
        page_list,
        me_ref,
        new_keys,
        new_values,
        pool_keys,
        pool_values,
    )
    w_other = core_swap(o_weight, n)
    q = queries.reshape(rows, qheads * width)
    cfg = (n, rows, kvheads, group, width, page, slots, kept)
    live = jnp.sum(
        (page_list // slots)[None, :] == jnp.arange(n, dtype=jnp.int32)[:, None], axis=1
    ).astype(jnp.int32)

    def look(step, here, state):
        blocks = []
        for d, pieces in here.items():
            blocks.append((d, 0, pieces))
            blocks.append((d, 1, [core_swap(p, n) for p in pieces]))
        return attend(cfg, live, me_ref, q, payload, blocks, state, step == sites // 2)

    (attended,) = ring_walk(payload, sites, look)

    if heads != 2 or sites % 2:
        parts = {}

        def multiply(step, here, _):
            for d, pieces in here.items():
                (part,) = product(spots, pieces, o_weight, w_other, 0)
                parts[d] = lax.ppermute(part, "ctx", site_perm(sites, -d)) if d else part
            return part

        ring_walk(attended, sites, multiply)
        order = jnp.stack(
            [jnp.mod(place_of(jnp.int32(s), sites) - place, sites) for s in range(sites)]
        )
        full = jnp.take(jnp.stack([parts[d] for d in range(sites)], axis=0), order, axis=0)
        full = full.transpose(1, 0, 2).reshape(rows, sites * CORES * cols)
        return lax.psum_scatter(full, "head", scatter_dimension=1, tiled=True)

    both = ("ctx", "head")
    arrived = {}

    last = sites // 2
    summing, crossing = [], []

    def swap_heads(x):
        return lax.ppermute(x, "head", [(0, 1), (1, 0)])

    def halves(d, keep, got):
        total = (keep + got.astype(jnp.float32)).astype(jnp.bfloat16)
        half = total.shape[0] // 2
        return total, ((d, total[:half]), (sites - d, total[half:]))

    def cross(after):
        got = swap_heads(join([p for _, *pair in crossing for p in pair], after))
        for i, (d, first, second) in enumerate(crossing):
            half = first.shape[0]
            arrived[d] = [(first, 0), (got, 2 * i * half)]
            arrived[sites - d] = [(second, 0), (got, (2 * i + 1) * half)]

    def multiply(step, here, _):
        if step in (0, last):
            (part,) = product(spots, here[step], o_weight, w_other, 0)
            if summing:
                d, keep, got = summing
                keep, got, part = lax.optimization_barrier((keep, got, part))
            within, across = back_perms(sites, heads, step)
            first = lax.ppermute(part, both, within) if step else part
            arrived[step] = [(first, 0), (lax.ppermute(part, both, across), 0)]
            if crossing:
                cross(part)
            if summing:
                for at, piece in halves(d, keep, got)[1]:
                    arrived[at] = [
                        (lax.ppermute(piece, both, perm), 0)
                        for perm in back_perms(sites, heads, at)
                    ]
            return [part, arrived[0][1][0]] if step == 0 else [part]
        keep, sent = product(spots, here[step] + here[sites - step], o_weight, w_other, heads)
        got = swap_heads(sent)
        if step == last - 1:
            summing.extend((step, keep, got))
            return [sent]
        total, pieces = halves(step, keep, got)
        back = [lax.ppermute(p, "ctx", site_perm(sites, -at)) for at, p in pieces]
        crossing.append((step, *back))
        return [total]

    ring_walk(attended, sites, multiply)
    operands, spans = [], []
    for d in range(sites):
        spans.append([(len(operands) + i, off) for i, (_, off) in enumerate(arrived[d])])
        operands += [x for x, _ in arrived[d]]
    return pl.pallas_call(
        functools.partial(assemble_kernel, sites, heads, spans),
        out_shape=jax.ShapeDtypeStruct((rows, sites * CORES * cols // heads), jnp.bfloat16),
        in_specs=[smem] + [vmem] * len(operands),
        out_specs=vmem,
        compiler_params=pltpu.CompilerParams(vmem_limit_bytes=SMALL_LIMIT),
        cost_estimate=FREE,
        name="assemble",
    )(spots, *operands)


def solution(mesh):
    n, heads = mesh.shape["ctx"], mesh.shape["head"]
    in_specs = (
        P("ctx", "head", None),
        P("ctx", "head", None),
        P("ctx", "head", None),
        P("ctx", None, "head", None),
        P("ctx", None, "head", None),
        P("head", "ctx"),
        P(),
    )
    out_specs = P("ctx", "head")
    return jax.shard_map(
        functools.partial(on_device, n, heads),
        mesh=mesh,
        in_specs=in_specs,
        out_specs=out_specs,
        check_vma=False,
    )
```

```python
import functools
import math

import jax
import jax.numpy as jnp
from jax import lax
from jax.experimental import pallas as pl
from jax.experimental.pallas import tpu as pltpu
from jax.sharding import PartitionSpec as P

CORES = 2
LINES = 2
NEG = -1e30
VMEM_LIMIT = 24 * 1024 * 1024
SMALL_LIMIT = 12 * 1024 * 1024
FREE = pl.CostEstimate(flops=0, bytes_accessed=0, transcendentals=0)


def cycle_of(sites):
    length = sites // LINES
    order = []
    for line in range(LINES):
        steps = range(length) if line % 2 == 0 else range(length - 1, -1, -1)
        order += [z * LINES + line for z in steps]
    return order


def place_of(site, sites):
    z, line = site // LINES, site % LINES
    length = sites // LINES
    return jnp.where(line == 0, z, 2 * length - 1 - z)


def site_perm(sites, shift):
    order = cycle_of(sites)
    return [
        (order[i] * CORES + k, order[(i + shift) % sites] * CORES + k)
        for i in range(sites)
        for k in range(CORES)
    ]


def core_swap(x, count):
    return lax.ppermute(x, "ctx", [(i, i ^ 1) for i in range(count)])


def ring_walk(block, sites, work):
    steps = sites // 2
    here, done = {0: [block]}, None
    f = b = block
    for step in range(1, steps + 1):
        if step < steps or sites % 2:
            f = lax.ppermute(f, "ctx", site_perm(sites, 1))
            b = lax.ppermute(b, "ctx", site_perm(sites, -1))
            arrived = {step: [f], sites - step: [b]}
        else:
            half = block.shape[0] // 2
            f = lax.ppermute(f[:half], "ctx", site_perm(sites, 1))
            b = lax.ppermute(b[half:], "ctx", site_perm(sites, -1))
            arrived = {step: [f, b]}
        done = work(step - 1, here, done)
        f, b, done = lax.optimization_barrier((f, b, done))
        here = {d: [f, b] if len(p) == 2 else [f] if d == step else [b] for d, p in arrived.items()}
    return work(steps, here, done)


def pack_kernel(slots, pages_ref, me_ref, nk_ref, nv_ref, pk_ref, pv_ref, out_ref):
    rows = nk_ref.shape[0]
    page = pk_ref.shape[1]
    kept = (out_ref.shape[0] // 2 - rows) // page
    half = out_ref.shape[0] // 2
    out_ref[...] = jnp.zeros_like(out_ref)
    heads, width = nk_ref.shape[1:]
    for h in range(heads):
        lanes = slice(h * width, (h + 1) * width)
        out_ref[0:rows, lanes] = nk_ref[:, h, :]
        out_ref[half : half + rows, lanes] = nv_ref[:, h, :]
    me = me_ref[0]

    def one(p, count):
        local = pages_ref[p] - me * slots
        mine = jnp.logical_and(local >= 0, local < slots)

        @pl.when(jnp.logical_and(mine, count < kept))
        def _():
            at = pl.multiple_of(rows + count * page, page)
            for h in range(heads):
                lanes = slice(h * width, (h + 1) * width)
                out_ref[pl.ds(at, page), lanes] = pk_ref[local, :, h, :]
                out_ref[pl.ds(pl.multiple_of(half + at, page), page), lanes] = pv_ref[
                    local, :, h, :
                ]

        return count + mine.astype(jnp.int32)

    lax.fori_loop(0, pages_ref.shape[0], one, jnp.int32(0))


def attend_kernel(cfg, first, last, counts, me_ref, q_ref, own_ref, ins, state, outs, scratch):
    n, rows, kvheads, group, width, page, slots, kept = cfg
    kbuf, vbuf, sbuf, dup, sem = scratch
    sites = n // CORES
    length = sites // LINES
    span = rows + kept * page
    total_keys = kbuf.shape[0]
    me = me_ref[0]
    my_site, my_core = me // CORES, me % CORES
    my_place = jnp.where(my_site % LINES == 0, my_site // LINES, 2 * length - 1 - my_site // LINES)

    pair = math.gcd(group, 4)
    tall = pair * rows
    steps = kvheads * group // pair
    scale = math.log2(math.e) * width ** (-0.5)
    chunk = CORES * span

    copies = [pltpu.make_async_copy(own_ref.at[0:16], dup, sem)]
    for b, (_, _, k_ref, k_at, v_ref, v_at) in enumerate(ins):
        at = pl.ds(b * span, span)
        copies.append(pltpu.make_async_copy(k_ref.at[pl.ds(k_at, span)], kbuf.at[at], sem))
        for h in range(kvheads):
            copies.append(
                pltpu.make_async_copy(
                    v_ref.at[pl.ds(v_at, span), pl.ds(h * width, width)],
                    vbuf.at[at, pl.ds(2 * h * width, width)],
                    sem,
                )
            )
    for copy in copies:
        copy.start()
    for h in range(kvheads):
        vbuf[:, (2 * h + 1) * width : (2 * h + 2) * width] = jnp.ones(
            (total_keys, width), jnp.bfloat16
        )
    for copy in copies:
        copy.wait()

    seen_key = dup[0:1, :]
    for b, (d, swap, *_) in enumerate(ins):
        place = lax.rem(my_place + sites - d, sites)
        line = place // length
        z = jnp.where(line == 0, place, 2 * length - 1 - place)
        owner = (z * LINES + line) * CORES + lax.rem(my_core + swap, CORES)

        def blank(at, size):
            kbuf[at : at + size, :] = jnp.broadcast_to(seen_key, (size, kbuf.shape[1]))
            vbuf[at : at + size, :] = jnp.zeros((size, vbuf.shape[1]), jnp.bfloat16)

        @pl.when(owner > me)
        def _():
            blank(b * span, rows)

        for j in range(kept):

            @pl.when(j >= counts[owner])
            def _():
                blank(b * span + rows + j * page, page)

    def lanes(i):
        return pl.ds(pl.multiple_of(i * width, width), width)

    def scores(i, slot):
        h = i // (group // pair)
        q = jnp.concatenate([q_ref[:, lanes(i * pair + g)] for g in range(pair)], axis=0)
        top = jnp.full((tall, width), NEG, jnp.float32)
        for j in range(total_keys // chunk):
            k = kbuf[j * chunk : (j + 1) * chunk, lanes(h)]
            s = lax.dot_general(q, k, (((1,), (1,)), ((), ())), preferred_element_type=jnp.float32)
            for a in range(chunk // width):
                piece = s[:, a * width : (a + 1) * width]
                at = j * chunk + a * width
                if first and at < rows:
                    row = lax.broadcasted_iota(jnp.int32, (rows, width), 0)
                    col = lax.broadcasted_iota(jnp.int32, (rows, width), 1) + at
                    seen = jnp.concatenate([col <= row] * pair, axis=0)
                    piece = jnp.where(seen, piece, NEG)
                sbuf[slot, :, at : at + width] = piece
                top = jnp.maximum(top, piece)
        return top

    def weigh(i, slot, top):
        h = i // (group // pair)
        at = pl.ds(pl.multiple_of(i * tall, tall), tall)
        best = jnp.max(top, axis=1, keepdims=True)
        if not first:
            was = state[1][at, 0:1]
            best = jnp.maximum(best, was)
        shift = best * scale
        acc = None
        for j in range(total_keys // chunk):
            s = sbuf[slot, :, j * chunk : (j + 1) * chunk]
            w = jnp.exp2(s * scale - shift).astype(jnp.bfloat16)
            v = vbuf[
                j * chunk : (j + 1) * chunk, pl.ds(pl.multiple_of(2 * h * width, width), 2 * width)
            ]
            part = jnp.dot(w, v, preferred_element_type=jnp.float32)
            acc = part if acc is None else acc + part
        mixed, total = acc[:, :width], acc[:, width:]
        if not first:
            left = jnp.exp2(was * scale - shift)
            mixed = mixed + state[0][at, :] * left
            total = total + state[1][at, width // 2 : width // 2 + 1] * left
        if last:
            out = (mixed / total).astype(jnp.bfloat16)
            for g in range(pair):
                outs[0][:, lanes(i * pair + g)] = out[g * rows : (g + 1) * rows]
        else:
            lane = lax.broadcasted_iota(jnp.int32, (tall, width), 1)
            outs[0][at, :] = mixed
            outs[1][at, :] = jnp.where(lane < width // 2, best, total)

    top = scores(0, 0)

    def two(t, top):
        after = scores(2 * t + 1, 1)
        weigh(2 * t, 0, top)
        top = scores(jnp.minimum(2 * t + 2, steps - 1), 0)
        weigh(2 * t + 1, 1, after)
        return top

    lax.fori_loop(0, steps // 2, two, top)


def attend(cfg, live, me_ref, queries, payload, blocks, state, last):
    n, rows, kvheads, group, width, page, slots, kept = cfg
    span = rows + kept * page
    smem = pl.BlockSpec(memory_space=pltpu.SMEM)
    vmem = pl.BlockSpec(memory_space=pltpu.VMEM)
    hbm = pl.BlockSpec(memory_space=pl.ANY)
    operands, spots = [], []
    for d, swap, pieces in blocks:
        base = len(operands)
        operands += pieces
        one = len(pieces) == 1
        spots.append((d, swap, base, 0, base if one else base + 1, span if one else 0))
    first = state is None
    state = [] if first else list(state)
    total_keys = len(blocks) * span
    tall = math.gcd(group, 4) * rows
    qrows = rows * kvheads * group
    if last:
        out_shape = [jax.ShapeDtypeStruct((rows, kvheads * group * width), jnp.bfloat16)]
    else:
        out_shape = [jax.ShapeDtypeStruct((qrows, width), jnp.float32)] * 2

    def body(live_ref, me_ref, q_ref, own_ref, *refs):
        ins = [(d, swap, refs[a], b, refs[c], e) for d, swap, a, b, c, e in spots]
        rest = refs[len(operands) :]
        held, rest = rest[: len(state)], rest[len(state) :]
        outs, scratch = rest[: len(out_shape)], rest[len(out_shape) :]
        attend_kernel(
            cfg, first, last, live_ref, me_ref, q_ref, own_ref, ins, held, outs, scratch
        )

    return pl.pallas_call(
        body,
        out_shape=out_shape,
        in_specs=[smem, smem, vmem, hbm] + [hbm] * len(operands) + [vmem] * len(state),
        out_specs=[vmem] * len(out_shape),
        scratch_shapes=[
            pltpu.VMEM((total_keys, kvheads * width), jnp.bfloat16),
            pltpu.VMEM((total_keys, 2 * kvheads * width), jnp.bfloat16),
            pltpu.VMEM((2, tall, total_keys), jnp.float32),
            pltpu.VMEM((16, kvheads * width), jnp.bfloat16),
            pltpu.SemaphoreType.DMA,
        ],
        compiler_params=pltpu.CompilerParams(vmem_limit_bytes=VMEM_LIMIT),
        cost_estimate=pl.CostEstimate(
            flops=4 * qrows * width * total_keys, bytes_accessed=0, transcendentals=0
        ),
        name="attend_last" if last else "attend",
    )(live, me_ref, queries, payload, *operands, *state)


def product(spots, pieces, own, other, split):
    depth, cols = own.shape
    tile = min(256, cols)
    half = cols // tile
    rows = sum(p.shape[0] for p in pieces)
    heads, blocks = (split, len(pieces)) if split else (1, 1)
    part = rows // blocks // heads
    assert heads <= 2

    def body(spots_ref, *refs):
        a_refs, rest = refs[: len(pieces)], refs[len(pieces) :]
        own_ref, other_ref, *outs = rest
        core, head = spots_ref[0], spots_ref[1]
        a = jnp.concatenate([r[...] for r in a_refs], axis=0)
        for t in range(2 * half):
            w_ref = own_ref if t < half else other_ref
            at = pl.multiple_of(lax.rem(t + half * core, 2 * half) * tile, tile)
            lanes = pl.ds(at, tile)
            columns = slice((t % half) * tile, (t % half + 1) * tile)
            out = jnp.dot(a, w_ref[:, columns], preferred_element_type=jnp.float32)
            if not split:
                outs[0][:, lanes] = out.astype(jnp.bfloat16)
                continue
            keep_ref, sent_ref, acc = outs
            acc[...] = out
            for b in range(blocks):
                mine = pl.ds(pl.multiple_of((b * heads + head) * part, part), part)
                rest = pl.ds(pl.multiple_of((b * heads + 1 - head) * part, part), part)
                keep_ref[b * part : (b + 1) * part, lanes] = acc[mine, :]
                sent_ref[b * part : (b + 1) * part, lanes] = acc[rest, :].astype(jnp.bfloat16)

    shape = (rows // heads, 2 * cols)
    outs = [jax.ShapeDtypeStruct(shape, jnp.bfloat16)]
    if split:
        outs = [jax.ShapeDtypeStruct(shape, jnp.float32)] + outs
    vmem = pl.BlockSpec(memory_space=pltpu.VMEM)
    return pl.pallas_call(
        body,
        out_shape=outs,
        in_specs=[pl.BlockSpec(memory_space=pltpu.SMEM)] + [vmem] * (len(pieces) + 2),
        out_specs=[vmem] * len(outs),
        scratch_shapes=[pltpu.VMEM((rows, tile), jnp.float32)] if split else [],
        compiler_params=pltpu.CompilerParams(vmem_limit_bytes=VMEM_LIMIT),
        cost_estimate=pl.CostEstimate(
            flops=4 * rows * depth * cols, bytes_accessed=0, transcendentals=0
        ),
        name="product",
    )(spots, *pieces, own, other)


def back_perms(sites, heads, shift):
    order = cycle_of(sites)
    within, across = [], []
    for i in range(sites):
        source, target = order[i], order[(i - shift) % sites]
        goal = source * heads // sites
        for k in range(CORES):
            for h in range(heads):
                pair = ((source * CORES + k) * heads + h, (target * CORES + k) * heads + goal)
                (within if h == goal else across).append(pair)
    return within, across


def assemble_kernel(sites, heads, spans, spots_ref, *refs):
    ins, out_ref = refs[:-1], refs[-1]
    length = sites // LINES
    rows = out_ref.shape[0]
    cols = out_ref.shape[1] * heads // sites
    part = rows // heads
    place, head = spots_ref[2], spots_ref[1]
    for d in range(sites):
        at = lax.rem(place + d, sites)
        line = at // length
        z = jnp.where(line == 0, at, 2 * length - 1 - at)
        site = z * LINES + line
        (first, first_at), (second, second_at) = [(ins[i], off) for i, off in spans[d]]

        @pl.when(site * heads // sites == head)
        def _():
            lanes = pl.ds(pl.multiple_of((site - head * (sites // heads)) * cols, cols), cols)
            if d in (0, sites // 2):
                total = first[...].astype(jnp.float32) + second[...].astype(jnp.float32)
                out_ref[:, lanes] = total.astype(jnp.bfloat16)
            else:
                mine = pl.ds(pl.multiple_of(head * part, part), part)
                other = pl.ds(pl.multiple_of((1 - head) * part, part), part)
                out_ref[mine, lanes] = first[first_at : first_at + part, :]
                out_ref[other, lanes] = second[second_at : second_at + part, :]


def join_kernel(count, *refs):
    refs[-1][...] = jnp.concatenate([r[...] for r in refs[:count]], axis=0)


def join(pieces, after):
    vmem = pl.BlockSpec(memory_space=pltpu.VMEM)
    rows = sum(p.shape[0] for p in pieces)
    return pl.pallas_call(
        functools.partial(join_kernel, len(pieces)),
        out_shape=jax.ShapeDtypeStruct((rows, pieces[0].shape[1]), pieces[0].dtype),
        in_specs=[vmem] * len(pieces) + [pl.BlockSpec(memory_space=pl.ANY)],
        out_specs=vmem,
        compiler_params=pltpu.CompilerParams(vmem_limit_bytes=SMALL_LIMIT),
        cost_estimate=FREE,
        name="join",
    )(*pieces, after)


def on_device(n, heads, queries, new_keys, new_values, pool_keys, pool_values, o_weight, page_list):
    rows, qheads, width = queries.shape
    kvheads = new_keys.shape[1]
    group = qheads // kvheads
    slots, page = pool_keys.shape[:2]
    npages = page_list.shape[0]
    kept = min(slots, 2 * npages // n)
    wide = kvheads * width
    sites = n // CORES
    cols = o_weight.shape[1]
    me = lax.axis_index("ctx")
    head = lax.axis_index("head")
    me_ref = me.reshape(1)
    place = place_of(me // CORES, sites)
    spots = jnp.stack([me % CORES, head, place]).astype(jnp.int32)
    smem = pl.BlockSpec(memory_space=pltpu.SMEM)
    vmem = pl.BlockSpec(memory_space=pltpu.VMEM)
    hbm = pl.BlockSpec(memory_space=pl.ANY)

    half = rows + kept * page
    payload = pl.pallas_call(
        functools.partial(pack_kernel, slots),
        out_shape=jax.ShapeDtypeStruct((2 * half, wide), jnp.bfloat16),
        in_specs=[smem, smem, vmem, vmem, vmem, vmem],
        out_specs=vmem,
        cost_estimate=FREE,
        name="pack_pages",
    )(
        page_list,
        me_ref,
        new_keys,
        new_values,
        pool_keys,
        pool_values,
    )
    w_other = core_swap(o_weight, n)
    q = queries.reshape(rows, qheads * width)
    cfg = (n, rows, kvheads, group, width, page, slots, kept)
    live = jnp.sum(
        (page_list // slots)[None, :] == jnp.arange(n, dtype=jnp.int32)[:, None], axis=1
    ).astype(jnp.int32)

    def look(step, here, state):
        blocks = []
        for d, pieces in here.items():
            blocks.append((d, 0, pieces))
            blocks.append((d, 1, [core_swap(p, n) for p in pieces]))
        return attend(cfg, live, me_ref, q, payload, blocks, state, step == sites // 2)

    (attended,) = ring_walk(payload, sites, look)

    if heads != 2 or sites % 2:
        parts = {}

        def multiply(step, here, _):
            for d, pieces in here.items():
                (part,) = product(spots, pieces, o_weight, w_other, 0)
                parts[d] = lax.ppermute(part, "ctx", site_perm(sites, -d)) if d else part
            return part

        ring_walk(attended, sites, multiply)
        order = jnp.stack(
            [jnp.mod(place_of(jnp.int32(s), sites) - place, sites) for s in range(sites)]
        )
        full = jnp.take(jnp.stack([parts[d] for d in range(sites)], axis=0), order, axis=0)
        full = full.transpose(1, 0, 2).reshape(rows, sites * CORES * cols)
        return lax.psum_scatter(full, "head", scatter_dimension=1, tiled=True)

    both = ("ctx", "head")
    arrived = {}

    last = sites // 2
    summing, crossing = [], []

    def swap_heads(x):
        return lax.ppermute(x, "head", [(0, 1), (1, 0)])

    def halves(d, keep, got):
        total = (keep + got.astype(jnp.float32)).astype(jnp.bfloat16)
        half = total.shape[0] // 2
        return total, ((d, total[:half]), (sites - d, total[half:]))

    def cross(after):
        got = swap_heads(join([p for _, *pair in crossing for p in pair], after))
        for i, (d, first, second) in enumerate(crossing):
            half = first.shape[0]
            arrived[d] = [(first, 0), (got, 2 * i * half)]
            arrived[sites - d] = [(second, 0), (got, (2 * i + 1) * half)]

    def multiply(step, here, _):
        if step in (0, last):
            (part,) = product(spots, here[step], o_weight, w_other, 0)
            if summing:
                d, keep, got = summing
                keep, got, part = lax.optimization_barrier((keep, got, part))
            within, across = back_perms(sites, heads, step)
            first = lax.ppermute(part, both, within) if step else part
            arrived[step] = [(first, 0), (lax.ppermute(part, both, across), 0)]
            if crossing:
                cross(part)
            if summing:
                for at, piece in halves(d, keep, got)[1]:
                    arrived[at] = [
                        (lax.ppermute(piece, both, perm), 0)
                        for perm in back_perms(sites, heads, at)
                    ]
            return [part, arrived[0][1][0]] if step == 0 else [part]
        keep, sent = product(spots, here[step] + here[sites - step], o_weight, w_other, heads)
        got = swap_heads(sent)
        if step == last - 1:
            summing.extend((step, keep, got))
            return [sent]
        total, pieces = halves(step, keep, got)
        back = [lax.ppermute(p, "ctx", site_perm(sites, -at)) for at, p in pieces]
        crossing.append((step, *back))
        return [total]

    ring_walk(attended, sites, multiply)
    operands, spans = [], []
    for d in range(sites):
        spans.append([(len(operands) + i, off) for i, (_, off) in enumerate(arrived[d])])
        operands += [x for x, _ in arrived[d]]
    return pl.pallas_call(
        functools.partial(assemble_kernel, sites, heads, spans),
        out_shape=jax.ShapeDtypeStruct((rows, sites * CORES * cols // heads), jnp.bfloat16),
        in_specs=[smem] + [vmem] * len(operands),
        out_specs=vmem,
        compiler_params=pltpu.CompilerParams(vmem_limit_bytes=SMALL_LIMIT),
        cost_estimate=FREE,
        name="assemble",
    )(spots, *operands)


def solution(mesh):
    n, heads = mesh.shape["ctx"], mesh.shape["head"]
    in_specs = (
        P("ctx", "head", None),
        P("ctx", "head", None),
        P("ctx", "head", None),
        P("ctx", None, "head", None),
        P("ctx", None, "head", None),
        P("head", "ctx"),
        P(),
    )
    out_specs = P("ctx", "head")
    return jax.shard_map(
        functools.partial(on_device, n, heads),
        mesh=mesh,
        in_specs=in_specs,
        out_specs=out_specs,
        check_vma=False,
    )
```
